256 devices in a mesh: slide: 16 (over z, core), seg: 16 (over x, y).
Axes of the slice: x: 4, y: 4, z: 8, core: 2. Of those that a mesh axis runs over, the one named last changes fastest.
Arguments:
- tissue_counts: int32 [16], P('slide'), may hold values from 4096 to 8192, as said below
- block_moves: int32 [16, 16, 2, 4], P('slide', 'seg'), may hold values from 0 to 15, as said below
- queries: bfloat16 [16, 8192, 768], P('slide', 'seg'), may hold values from -6 to 6
- key_rows: bfloat16 [16, 8192, 768], P('slide', 'seg'), may hold values from -6 to 6
- values: bfloat16 [16, 8192, 768], P('slide', 'seg'), may hold values from -6 to 6
- forward_out: bfloat16 [16, 8192, 768], P('slide', 'seg'), may hold values from -3 to 3
- log_norms: float32 [16, 12, 8192], P('slide', None, 'seg'), may hold values from 7 to 9
- out_grads: bfloat16 [16, 8192, 768], P('slide', 'seg'), may hold values from -288 to 288
- proj_weights: bfloat16 [768, 2304], replicated, may hold values from -0.21875 to 0.21875
Outputs:
- packed_grads: bfloat16 [16, 8192, 768], P('slide', 'seg')
The draws below stay inside these ranges and needn't reach their ends.
Inputs may be any that keep to these rules, and one draw needn't show every extreme that they name: Tissue tiles of each slide; the first tissue_counts[s] positions of slide s are tissue, the rest padding. One slide is full in every draw. Slot t of device (d, j) of the packed layout holds block block_moves[d, j, 1, t] of slide block_moves[d, j, 0, t] at the same seg index j, or is empty when that block index is 4. Each block that holds a position below its slide's tissue count sits in exactly one slot; no other block sits in any. One device of the packed layout holds at most 1 block of one slide, and some device holds 1 block of some slide.
All inputs are finite; a program needn't handle non-finite values.
Results may differ from the reference program's by a relative error of at most 0.0058.
Values may be sent and summed in bfloat16 or wider, within the bound.
A program may use at most 128 MiB of HBM per device.

```python
import jax
import jax.numpy as jnp
from jax import lax

D = 768
H = 12
W1 = 512
R = 16
BLK = 128
S_DEV = 512
SEQ = 8192
SLIDES = 16
NB = 4


def tile_counts(key):
    lowest = SEQ // 2
    spread = jax.random.randint(key, (SLIDES,), 0, 4097)
    drawn = lowest + (SEQ - lowest) * spread // 4096
    full_slide = jax.random.randint(jax.random.fold_in(key, 11), (), 0, SLIDES)
    return jnp.where(jnp.arange(SLIDES) == full_slide, SEQ, drawn).astype(jnp.int32)


def draw_tissue_counts(key, part):
    return tile_counts(key)


def draw_block_moves(key, part):
    counts = tile_counts(key)
    key = jax.random.fold_in(key, 3)
    seg_count = SEQ // S_DEV
    block_count = S_DEV // BLK
    blocks_live = (counts + BLK - 1) // BLK
    order = jnp.arange(seg_count)[:, None, None] * block_count + jnp.arange(block_count)[None, None, :]
    alive = order < blocks_live[None, :, None]
    flat = alive.reshape(seg_count, SLIDES * block_count).astype(jnp.int32)
    ranks = (jnp.cumsum(flat, axis=1) - flat).reshape(seg_count, SLIDES, block_count)
    holders = jax.vmap(lambda subkey: jax.random.permutation(subkey, SLIDES))(jax.random.split(key, seg_count))
    slot_orders = jax.vmap(lambda subkey: jax.random.permutation(subkey, block_count))(jax.random.split(jax.random.fold_in(key, 5), seg_count * SLIDES)).reshape(seg_count, SLIDES, block_count)
    column = jnp.broadcast_to(jnp.arange(seg_count)[:, None, None], ranks.shape)
    holder = jnp.take_along_axis(holders, (ranks % SLIDES).reshape(seg_count, -1), axis=1).reshape(ranks.shape)
    slot = slot_orders[column, holder, jnp.minimum(ranks // SLIDES, block_count - 1)]
    target = jnp.where(alive, holder, SLIDES)
    source = jnp.broadcast_to(jnp.arange(SLIDES)[None, :, None], ranks.shape).astype(jnp.int32)
    block = jnp.broadcast_to(jnp.arange(block_count)[None, None, :], ranks.shape).astype(jnp.int32)
    source_table = jnp.broadcast_to(jnp.arange(SLIDES)[:, None, None], (SLIDES, seg_count, block_count)).astype(jnp.int32)
    block_table = jnp.full((SLIDES, seg_count, block_count), block_count, jnp.int32)
    source_table = source_table.at[target, column, slot].set(source, mode='drop')
    block_table = block_table.at[target, column, slot].set(block, mode='drop')
    return jnp.stack([source_table, block_table], axis=2).astype(jnp.int32)


def shard_levels(rng, extent, cuts, smallest, high):
    gain, own = 1.0, jax.random.fold_in(rng, 6)
    for dim, blocks in cuts:
        draws = jnp.exp(jax.random.uniform(jax.random.fold_in(own, dim), (blocks,), jnp.float32, smallest / len(cuts), high / len(cuts)))
        gain = gain * jnp.repeat(draws, extent[dim] // blocks).reshape([-1 if axis == dim else 1 for axis in range(len(extent))])
    return gain


def bell_draw(rng, shape, scale, reach, pieces=(), dtype=jnp.bfloat16):
    gain = shard_levels(rng, shape, pieces, -0.22, 0.18) if pieces else 1.0
    result = jax.random.normal(rng, shape, jnp.float32) * scale * gain
    return jnp.minimum(jnp.maximum(result, -reach), reach).astype(dtype)


def setup_inputs(seed: int = 0) -> dict:
    arg_keys = jax.random.split(jax.random.key(seed), 10)
    return {
        "tissue_counts": draw_tissue_counts(jax.random.fold_in(arg_keys[9], 71), 0),
        "block_moves": draw_block_moves(jax.random.fold_in(arg_keys[9], 71), 0),
        "queries": bell_draw(arg_keys[2], (SLIDES, SEQ, D), 1.0, 6.0, ((0, 16), (1, 16))),
        "key_rows": bell_draw(arg_keys[3], (SLIDES, SEQ, D), 1.0, 6.0, ((0, 16), (1, 16))),
        "values": bell_draw(arg_keys[4], (SLIDES, SEQ, D), 1.0, 6.0, ((0, 16), (1, 16))),
        "forward_out": bell_draw(arg_keys[5], (SLIDES, SEQ, D), 0.5, 3.0, ((0, 16), (1, 16))),
        "log_norms": jnp.clip(7.0 + 2.0 * jax.random.uniform(arg_keys[6], (SLIDES, H, SEQ), jnp.float32) ** shard_levels(arg_keys[6], (SLIDES, H, SEQ), ((0, 16), (2, 16)), -0.2, 0.2), 7.0, 9.0),
        "out_grads": bell_draw(arg_keys[7], (SLIDES, SEQ, D), 48.0, 288.0, ((0, 16), (1, 16))),
        "proj_weights": bell_draw(arg_keys[8], (D, 3 * D), D ** -0.5, 0.21875),
    }


def widen(array):
    return array.astype(jnp.float32)


def rounded(array):
    return widen(lax.optimization_barrier(array.astype(jnp.bfloat16)))


def local_head(head_index, query_heads, key_heads, value_heads, grad_heads, norm_rows, dot_rows, row_alive):
    segments = SEQ // W1
    head_size = D // H
    scaling = head_size ** -0.5
    query_part = query_heads[:, head_index, :].reshape(segments, W1, head_size)
    key_part = key_heads[:, head_index, :].reshape(segments, W1, head_size)
    value_part = value_heads[:, head_index, :].reshape(segments, W1, head_size)
    grad_part = grad_heads[:, head_index, :].reshape(segments, W1, head_size)
    norm_part = norm_rows[head_index].reshape(segments, W1)
    dot_part = dot_rows[head_index].reshape(segments, W1)
    scores = jnp.einsum('nqd,nkd->nqk', query_part, key_part) * scaling
    weights = jnp.where(row_alive.reshape(segments, 1, W1), jnp.exp(scores - norm_part[:, :, None]), 0.0)
    grad_weights = jnp.einsum('nqd,nkd->nqk', grad_part, value_part)
    grad_scores = rounded(weights * (grad_weights - dot_part[:, :, None]))
    value_grad = jnp.einsum('nqk,nqd->nkd', rounded(weights), grad_part)
    key_grad = scaling * jnp.einsum('nqk,nqd->nkd', grad_scores, query_part)
    query_grad = scaling * jnp.einsum('nqk,nkd->nqd', grad_scores, key_part)
    return query_grad.reshape(SEQ, head_size), key_grad.reshape(SEQ, head_size), value_grad.reshape(SEQ, head_size)


def slide_grads(tile_limit, queries, key_rows, values, forward_out, log_norms, home_grads, proj_weights):
    head_size = D // H
    scaling = head_size ** -0.5
    positions = jnp.arange(SEQ)
    row_alive = positions < tile_limit
    home_grads = jnp.where(row_alive[:, None], home_grads, jnp.zeros_like(home_grads))
    query_heads = widen(queries).reshape(SEQ, H, head_size)
    key_heads = widen(key_rows).reshape(SEQ, H, head_size)
    value_heads = widen(values).reshape(SEQ, H, head_size)
    grad_heads = widen(home_grads).reshape(SEQ, H, head_size)
    out_heads = widen(forward_out).reshape(SEQ, H, head_size)
    dot_rows = jnp.einsum('phd,phd->hp', grad_heads, out_heads)
    local_query, local_key, local_value = lax.map(
        lambda head_index: local_head(head_index, query_heads, key_heads, value_heads, grad_heads, log_norms, dot_rows, row_alive),
        jnp.arange(H))
    head_ids = jnp.arange(H)
    sparse_pos = jnp.arange(SEQ // R)[:, None] * R + (head_ids % R)[None, :]
    query_sparse = query_heads[sparse_pos, head_ids]
    key_sparse = key_heads[sparse_pos, head_ids]
    value_sparse = value_heads[sparse_pos, head_ids]
    grad_sparse = grad_heads[sparse_pos, head_ids]
    norm_sparse = log_norms[head_ids[:, None], sparse_pos.T]
    dot_sparse = dot_rows[head_ids[:, None], sparse_pos.T]
    key_alive = (sparse_pos < tile_limit).T
    scores = jnp.einsum('qhd,khd->hqk', query_sparse, key_sparse) * scaling
    weights = jnp.where(key_alive[:, None, :], jnp.exp(scores - norm_sparse[:, :, None]), 0.0)
    grad_weights = jnp.einsum('qhd,khd->hqk', grad_sparse, value_sparse)
    grad_scores = rounded(weights * (grad_weights - dot_sparse[:, :, None]))
    sparse_value_grad = jnp.einsum('hqk,qhd->khd', rounded(weights), grad_sparse)
    sparse_key_grad = scaling * jnp.einsum('hqk,qhd->khd', grad_scores, query_sparse)
    sparse_query_grad = scaling * jnp.einsum('hqk,khd->qhd', grad_scores, key_sparse)

    def combine(local_part, sparse_part):
        dense = jnp.transpose(local_part, (1, 0, 2)).at[sparse_pos, head_ids].add(sparse_part)
        return dense.reshape(SEQ, D).astype(jnp.bfloat16)

    grad_query = combine(local_query, sparse_query_grad)
    grad_key = combine(local_key, sparse_key_grad)
    grad_value = combine(local_value, sparse_value_grad)
    mixed = jnp.dot(grad_query, proj_weights[:, :D].T, preferred_element_type=jnp.float32)
    mixed = mixed + jnp.dot(grad_key, proj_weights[:, D:2 * D].T, preferred_element_type=jnp.float32)
    mixed = mixed + jnp.dot(grad_value, proj_weights[:, 2 * D:].T, preferred_element_type=jnp.float32)
    return mixed.astype(jnp.bfloat16)


def reference(tissue_counts, block_moves, queries, key_rows, values, forward_out, log_norms, out_grads, proj_weights):
    seg_count = SEQ // S_DEV
    block_source = block_moves[:, :, 0, :]
    block_index = block_moves[:, :, 1, :]
    column = jnp.broadcast_to(jnp.arange(seg_count)[None, :, None], block_index.shape)
    packed = out_grads.reshape(SLIDES, seg_count, NB, BLK, D)
    home = jnp.zeros_like(packed).at[block_source, column, block_index].set(packed, mode="drop")
    home = home.reshape(SLIDES, SEQ, D)
    mixed = lax.map(
        lambda operands: slide_grads(operands[0], operands[1], operands[2], operands[3], operands[4], operands[5], operands[6], proj_weights),
        (tissue_counts, queries, key_rows, values, forward_out, log_norms, home))
    mixed = mixed.reshape(SLIDES, seg_count, NB, BLK, D)
    gathered = mixed[block_source, column, jnp.minimum(block_index, NB - 1)]
    filled = jnp.where((block_index < NB)[:, :, :, None, None], gathered, jnp.zeros_like(gathered))
    return filled.reshape(SLIDES, SEQ, D)
```

```python
import jax
import jax.numpy as jnp
from jax import lax
from jax.experimental import pallas as pl
from jax.experimental.pallas import tpu as pltpu
from jax.sharding import PartitionSpec as P

D = 768
H = 12
R = 16
BLK = 128
ROWS = 512
HS = D // H
LANES = 128
PAIRS = D // LANES
N = 16
CHUNKS = 3
HALF = D // 2
BF = jnp.bfloat16
F32 = jnp.float32
MESH = pl.DeviceIdType.MESH


def dot(a, b):
    return jnp.dot(a, b, preferred_element_type=F32)


def dot_nt(a, b):
    return lax.dot_general(a, b, (((1,), (1,)), ((), ())), preferred_element_type=F32)


def await_bytes(ref, sem):
    pltpu.make_async_copy(ref, ref, sem).wait()


def transposed(x):
    return jnp.transpose(x.astype(F32)).astype(BF)


def row_dots(ones, grads, outs):
    product = grads.astype(F32) * outs.astype(F32)
    high = product.astype(BF)
    low = (product - high.astype(F32)).astype(BF)
    return dot_nt(ones, high) + dot_nt(ones, low)


def attend(keys, vals, query, grad, keys_t, norm, dots):
    value_parts, key_parts, query_t = [], [], None
    for i in range(2):
        rows = slice(256 * i, 256 * i + 256)
        weights = jnp.exp(dot_nt(keys[rows], query) - norm)
        slopes = dot_nt(vals[rows], grad)
        scores = (weights * (slopes - dots)).astype(BF)
        value_parts.append(dot(weights.astype(BF), grad))
        key_parts.append(dot(scores, query))
        part = dot(keys_t[:, rows], scores)
        query_t = part if query_t is None else query_t + part
    return query_t, jnp.concatenate(key_parts, axis=0), jnp.concatenate(value_parts, axis=0)


def kernel(
    count_ref, moves_ref, q_hbm, k_hbm, v_hbm, o_hbm, norm_hbm, og_hbm, w_hbm, out_ref,
    qv, kv, vv, ov, nv, wv, k_t, tsend, trecv, tabv, tabs,
    r1a, r1b, r1c, s2, gbuf, em, ebuf, nmsg, nbuf, gm, gdbuf, rsend, rbuf, tmp, acc, xs, mix,
    q1a, q1b, q1c, t2, in_sem, p1s, p1r, p1l, p2s, p2r, p2l, o1s, o1r, o1l, o2s, o2r, o2l,
    ss, rs, ls,
):
    me = lax.axis_index("slide")
    seg = lax.axis_index("seg")
    my_z, my_c = me // 2, me % 2
    r1, q1 = (r1a, r1b, r1c), (q1a, q1b, q1c)

    loads = [
        pltpu.make_async_copy(src, dst, in_sem.at[i])
        for i, (src, dst) in enumerate(
            ((q_hbm, qv), (k_hbm, kv), (v_hbm, vv), (o_hbm, ov), (norm_hbm, nv), (w_hbm, wv))
        )
    ]
    for load in loads:
        load.start()

    barrier = pltpu.get_barrier_semaphore()

    def greet(r, carry):
        pl.semaphore_signal(
            barrier, inc=1, device_id={"slide": lax.rem(me + r, N)}, device_id_type=MESH
        )
        pl.semaphore_signal(
            barrier, inc=1, device_id={"seg": lax.rem(seg + r, N)}, device_id_type=MESH
        )
        return carry

    lax.fori_loop(1, N, greet, 0)

    lane = lax.broadcasted_iota(jnp.int32, (8, LANES), 1)
    sub = lax.broadcasted_iota(jnp.int32, (8, LANES), 0)
    table = jnp.zeros((8, LANES), jnp.int32)
    for t in range(4):
        block = moves_ref[1, t]
        code = jnp.where(block < 4, moves_ref[0, t] * 4 + block, 4 * N)
        table = jnp.where(sub == t, code, table)
        table = jnp.where((sub == 4) & (lane == me * 4 + t), code, table)
    tsend[...] = table
    trecv[pl.ds(me, 1)] = table.reshape(1, 8, LANES)
    for buf in r1 + q1:
        buf[64:68] = jnp.zeros((4, 16, LANES), BF)

    pl.semaphore_wait(barrier, 2 * (N - 1))

    def columns(core, k):
        return pl.ds(pl.multiple_of(core * HALF + k * LANES, LANES), LANES)

    def send_table(r, carry):
        dest = lax.rem(me + r, N)
        pltpu.make_async_remote_copy(
            tsend, trecv.at[me], ss.at[0], rs.at[0], device_id={"slide": dest}, device_id_type=MESH
        ).start()
        return carry

    def spread(k, buf, source, send_sem, recv_sem, local_sem):
        slot = buf.at[pl.ds(me * 4, 4)]

        def one(r, carry):
            dest = lax.rem(me + r, N)
            pltpu.make_async_remote_copy(
                source(dest), slot, send_sem.at[k], recv_sem.at[k],
                device_id={"slide": dest}, device_id_type=MESH,
            ).start()
            return carry

        lax.fori_loop(1, N, one, 0)
        pltpu.make_async_copy(source(me), slot, local_sem.at[k]).start()

    def deliver(k, buf, target, send_sem, recv_sem, local_sem):
        landing = target.at[:, my_z, :, columns(my_c, k)]

        def one(r, carry):
            dest = lax.rem(me + r, N)
            pltpu.make_async_remote_copy(
                buf.at[k, pl.ds(dest * 4, 4)], landing, send_sem.at[k], recv_sem.at[k],
                device_id={"slide": dest}, device_id_type=MESH,
            ).start()
            return carry

        lax.fori_loop(1, N, one, 0)
        pltpu.make_async_copy(buf.at[k, pl.ds(me * 4, 4)], landing, local_sem.at[k]).start()

    def arrived(k, recv_sem, local_sem):
        await_bytes(s2.at[0, pl.ds(0, 60)], recv_sem.at[k])
        await_bytes(s2.at[0, pl.ds(0, 4)], local_sem.at[k])

    def choose(k, row, source, target):
        def one(i, carry):
            target[k, i] = source[tabs[row, i]]
            return carry

        lax.fori_loop(0, 4 * N, one, 0, unroll=8)

    lax.fori_loop(1, N, send_table, 0)
    for k in range(CHUNKS):
        spread(
            k, r1[k], lambda dest, k=k: og_hbm.at[:, dest // 2, :, columns(dest % 2, k)],
            p1s, p1r, p1l,
        )

    for load in loads[:5]:
        load.wait()
    alive = (lax.broadcasted_iota(jnp.int32, (ROWS, LANES), 0) + seg * ROWS) < count_ref[0]
    first = lax.broadcasted_iota(jnp.int32, (32, LANES), 1) < HS

    def dilate(ref, pair):
        return jnp.where(
            first,
            ref[pl.ds(2 * pair, 32, stride=R), :],
            ref[pl.ds(2 * pair + 1, 32, stride=R), :],
        ).astype(BF)

    def prepare(pair, carry):
        cols = pl.ds(pl.multiple_of(pair * LANES, LANES), LANES)
        query = qv[:, cols].astype(F32) * (HS ** -0.5)
        keys = jnp.where(alive, kv[:, cols].astype(F32), 0.0)
        qv[:, cols] = query.astype(BF)
        kv[:, cols] = keys.astype(BF)
        k_t[pair] = jnp.transpose(keys).astype(BF)
        tmp[0] = query
        tmp[1] = keys
        tmp[2] = vv[:, cols].astype(F32)
        tmp[3] = ov[:, cols].astype(F32)
        for n in range(4):
            em[pair, n] = dilate(tmp.at[n], pair)
        return carry

    lax.fori_loop(0, PAIRS, prepare, 0)

    norms = nv[...]
    head_row = lax.broadcasted_iota(jnp.int32, (H, ROWS), 0)
    head_lane = lax.broadcasted_iota(jnp.int32, (H, ROWS), 1)
    rest = jnp.where(head_lane % R == head_row, norms, 0.0)
    fold_row = lax.broadcasted_iota(jnp.int32, (ROWS, LANES), 0)
    fold_lane = lax.broadcasted_iota(jnp.int32, (ROWS, LANES), 1)
    fold = jnp.where(fold_row // R + 32 * (seg % 4) == fold_lane, 1.0, 0.0).astype(BF)
    folded = jnp.zeros((H, LANES), F32)
    for _ in range(3):
        piece = rest.astype(BF)
        folded = folded + dot(piece, fold)
        rest = rest - piece.astype(F32)
    for h in range(H):
        nmsg[h] = jnp.broadcast_to(folded[h : h + 1], (8, LANES))

    def send_head(src, dst, index, head):
        @pl.when(head != seg)
        def _():
            pltpu.make_async_remote_copy(
                src, dst, ss.at[index], rs.at[index], device_id={"seg": head}, device_id_type=MESH
            ).start()

        @pl.when(head == seg)
        def _():
            pltpu.make_async_copy(src, dst, ls.at[index]).start()

    def send_early(r, carry):
        head = lax.rem(seg + r, N)

        @pl.when(head < H)
        def _():
            send_head(em.at[head // 2], ebuf.at[seg], 1, head)
            send_head(nmsg.at[head], nbuf.at[seg], 2, head)

        return carry

    lax.fori_loop(0, N, send_early, 0)

    await_bytes(trecv.at[pl.ds(0, N - 1)], rs.at[0])
    inverse = jnp.zeros((8, LANES), jnp.int32)
    codes = jnp.zeros((8, LANES), jnp.int32)
    for d in range(N):
        got = trecv[d]
        inverse = inverse + jnp.where((sub < 4) & (got == lane), d * 4 + sub - 4 * N, 0)
        codes = codes + got
    inverse = jnp.sum(inverse, axis=0, keepdims=True) + 4 * N
    tabv[...] = jnp.clip(jnp.where(sub == 0, inverse, codes), 0, 4 * N)
    table_copy = pltpu.make_async_copy(tabv, tabs, ls.at[0])
    table_copy.start()
    table_copy.wait()

    for k in range(CHUNKS):
        arrived(k, p1r, p1l)
        choose(k, 0, r1[k], s2)
        deliver(k, s2, gbuf, p2s, p2r, p2l)

    ones_row = lax.broadcasted_iota(jnp.int32, (8, LANES), 0)
    ones_half = lax.broadcasted_iota(jnp.int32, (8, LANES), 1) // HS
    pair_ones = jnp.where(ones_row == ones_half, 1.0, 0.0).astype(BF)
    wide_half = lax.broadcasted_iota(jnp.int32, (ROWS, LANES), 1) // HS

    def sparse_head():
        await_bytes(ebuf.at[pl.ds(0, N - 1)], rs.at[1])
        await_bytes(ebuf.at[0], ls.at[1])
        await_bytes(nbuf.at[pl.ds(0, N - 1)], rs.at[2])
        await_bytes(nbuf.at[0], ls.at[2])
        await_bytes(gdbuf.at[pl.ds(0, N - 1)], rs.at[3])
        await_bytes(gdbuf.at[0], ls.at[3])
        mine = wide_half == seg % 2
        zero = jnp.zeros((ROWS, LANES), BF)
        query = jnp.where(mine, ebuf[:, 0].reshape(ROWS, LANES), zero)
        keys = jnp.where(mine, ebuf[:, 1].reshape(ROWS, LANES), zero)
        vals = ebuf[:, 2].reshape(ROWS, LANES)
        outs = ebuf[:, 3].reshape(ROWS, LANES)
        grad = jnp.where(mine, gdbuf[...].reshape(ROWS, LANES), zero)
        norm = jnp.concatenate(
            [
                sum(nbuf[4 * part + i, 0:1, :] for i in range(4))
                for part in range(4)
            ],
            axis=1,
        )
        dots = row_dots(jnp.ones((8, LANES), BF), grad, outs)[0:1]
        query_t, key_sum, value_sum = attend(
            keys, vals, query, grad, transposed(keys), norm, dots
        )
        rsend[:, 0] = (jnp.transpose(query_t) * (HS ** -0.5)).astype(BF).reshape(N, 32, LANES)
        rsend[:, 1] = key_sum.astype(BF).reshape(N, 32, LANES)
        rsend[:, 2] = value_sum.astype(BF).reshape(N, 32, LANES)

        def back(r, carry):
            dest = lax.rem(seg + r, N)
            pltpu.make_async_remote_copy(
                rsend.at[dest], rbuf.at[seg], ss.at[4], rs.at[4],
                device_id={"seg": dest}, device_id_type=MESH,
            ).start()
            return carry

        lax.fori_loop(1, N, back, 0)
        pltpu.make_async_copy(rsend.at[seg], rbuf.at[seg], ls.at[4]).start()

    def chunk(k, carry):
        arrived(k, p2r, p2l)

        def share(u, inner):
            pair = u * CHUNKS + k
            cols = pl.ds(pl.multiple_of(pair * LANES, LANES), LANES)
            grad = jnp.where(alive, gbuf[:, :, :, cols].reshape(ROWS, LANES).astype(F32), 0.0)
            tmp[u] = grad
            gm[pair] = dilate(tmp.at[u], pair)
            send_head(gm.at[pair], gdbuf.at[seg], 3, 2 * pair)
            send_head(gm.at[pair], gdbuf.at[seg], 3, 2 * pair + 1)
            return inner

        lax.fori_loop(0, 2, share, 0)

        def local_pair(u, inner):
            pair = u * CHUNKS + k
            cols = pl.ds(pl.multiple_of(pair * LANES, LANES), LANES)
            query, keys, vals = qv[:, cols], kv[:, cols], vv[:, cols]
            grad = tmp[u].astype(BF)
            zero = jnp.zeros((ROWS, LANES), BF)
            dots = row_dots(pair_ones, grad, ov[:, cols])
            query_parts, key_sum, value_sum = [], None, None
            for x in range(2):
                mine = wide_half == x
                query_t, key_part, value_part = attend(
                    keys, vals, jnp.where(mine, query, zero), jnp.where(mine, grad, zero),
                    k_t[pair, x * HS : (x + 1) * HS, :],
                    nv[pl.ds(2 * pair + x, 1), :], dots[x : x + 1],
                )
                query_parts.append(query_t)
                key_sum = key_part if key_sum is None else key_sum + key_part
                value_sum = value_part if value_sum is None else value_sum + value_part
            acc[pair] = jnp.transpose(jnp.concatenate(query_parts, axis=0)) * (HS ** -0.5)
            acc[PAIRS + pair] = key_sum
            acc[2 * PAIRS + pair] = value_sum

            @pl.when((u == 0) & (seg < H) & ((seg // 2) % CHUNKS == k))
            def _():
                sparse_head()

            return inner

        lax.fori_loop(0, 2, local_pair, 0)
        return carry

    lax.fori_loop(0, CHUNKS, chunk, 0)

    @pl.when(seg < H)
    def _():
        await_bytes(rbuf.at[pl.ds(0, H - 1)], rs.at[4])
        await_bytes(rbuf.at[0], ls.at[4])

    @pl.when(seg >= H)
    def _():
        await_bytes(rbuf, rs.at[4])

    for n in range(3):
        for pair in range(PAIRS):
            place = acc.at[n * PAIRS + pair]
            for head in (2 * pair, 2 * pair + 1):
                rows = pl.ds(head, 32, stride=R)
                place[rows, :] = place[rows, :] + rbuf[head, n].astype(F32)
            xs[:, n * D + pair * LANES : n * D + (pair + 1) * LANES] = place[...].astype(BF)

    loads[5].wait()
    for k in range(CHUNKS):
        weights = jnp.concatenate(
            [wv[core * HALF + k * LANES : core * HALF + (k + 1) * LANES, :] for core in range(2)],
            axis=0,
        )
        mixed = dot_nt(xs[...], weights)
        for core in range(2):
            half = jnp.where(alive, mixed[:, core * LANES : (core + 1) * LANES], 0.0)
            mix[k, core] = half.astype(BF).reshape(4, 8, 16, LANES)
        spread(
            k, q1[k], lambda dest, k=k: mix.at[k, dest % 2, :, dest // 2], o1s, o1r, o1l
        )

    for k in range(CHUNKS):
        arrived(k, o1r, o1l)
        choose(k, 4, q1[k], t2)
        deliver(k, t2, out_ref, o2s, o2r, o2l)
    for k in range(CHUNKS):
        arrived(k, o2r, o2l)

    for sems in (p1s, p2s, o1s, o2s):
        for k in range(CHUNKS):
            await_bytes(s2.at[0, pl.ds(0, 60)], sems.at[k])
    await_bytes(trecv.at[pl.ds(0, N - 1)], ss.at[0])

    @pl.when(seg < H)
    def _():
        await_bytes(ebuf.at[pl.ds(0, H - 1)], ss.at[1])
        await_bytes(nbuf.at[pl.ds(0, H - 1)], ss.at[2])
        await_bytes(gdbuf.at[pl.ds(0, H - 1)], ss.at[3])
        await_bytes(rsend.at[pl.ds(0, N - 1)], ss.at[4])

    @pl.when(seg >= H)
    def _():
        await_bytes(ebuf.at[pl.ds(0, H)], ss.at[1])
        await_bytes(nbuf.at[pl.ds(0, H)], ss.at[2])
        await_bytes(gdbuf.at[pl.ds(0, H)], ss.at[3])


def shards(counts, moves, queries, key_rows, values, forward_out, log_norms, out_grads, weights):
    dma = pltpu.SemaphoreType.DMA
    vmem = pltpu.VMEM
    any_spec = pl.BlockSpec(memory_space=pl.ANY)
    smem_spec = pl.BlockSpec(memory_space=pltpu.SMEM)
    scratch = [
        *[vmem((ROWS, D), BF)] * 4,
        vmem((H, ROWS), F32),
        vmem((D, 3 * D), BF),
        vmem((PAIRS, LANES, ROWS), BF),
        vmem((8, LANES), jnp.int32),
        vmem((N, 8, LANES), jnp.int32),
        vmem((8, LANES), jnp.int32),
        pltpu.SMEM((8, LANES), jnp.int32),
        *[vmem((68, 16, LANES), BF)] * 3,
        vmem((CHUNKS, 64, 16, LANES), BF),
        vmem((4, 8, 16, D), BF),
        vmem((PAIRS, 4, 32, LANES), BF),
        vmem((N, 4, 32, LANES), BF),
        vmem((H, 8, LANES), F32),
        vmem((N, 8, LANES), F32),
        vmem((PAIRS, 32, LANES), BF),
        vmem((N, 32, LANES), BF),
        vmem((N, 3, 32, LANES), BF),
        vmem((H, 3, 32, LANES), BF),
        vmem((4, ROWS, LANES), F32),
        vmem((3 * PAIRS, ROWS, LANES), F32),
        vmem((ROWS, 3 * D), BF),
        vmem((CHUNKS, 2, 4, 8, 16, LANES), BF),
        *[vmem((68, 16, LANES), BF)] * 3,
        vmem((CHUNKS, 64, 16, LANES), BF),
        dma((6,)),
        *[dma((CHUNKS,))] * 12,
        *[dma((5,))] * 3,
    ]
    result = pl.pallas_call(
        kernel,
        out_shape=jax.ShapeDtypeStruct((4, 8, 16, D), BF),
        in_specs=[smem_spec, smem_spec] + [any_spec] * 7,
        out_specs=any_spec,
        scratch_shapes=scratch,
        compiler_params=pltpu.CompilerParams(
            collective_id=0, has_side_effects=True, vmem_limit_bytes=50 * 1024 * 1024
        ),
        name="dilated_backward",
    )(
        counts,
        moves[0, 0],
        queries[0],
        key_rows[0],
        values[0],
        forward_out[0],
        log_norms[0],
        out_grads[0].reshape(4, 8, 16, D),
        weights,
    )
    return result.reshape(1, ROWS, D)


def solution(mesh):
    return jax.shard_map(
        shards,
        mesh=mesh,
        in_specs=(
            P("slide"),
            P("slide", "seg", None, None),
            P("slide", "seg", None),
            P("slide", "seg", None),
            P("slide", "seg", None),
            P("slide", "seg", None),
            P("slide", None, "seg"),
            P("slide", "seg", None),
            P(),
        ),
        out_specs=P("slide", "seg", None),
        check_vma=False,
    )
```

```python
import jax
import jax.numpy as jnp
from jax import lax
from jax.experimental import pallas as pl
from jax.experimental.pallas import tpu as pltpu
from jax.sharding import PartitionSpec as P

D = 768
H = 12
R = 16
BLK = 128
ROWS = 512
HS = D // H
LANES = 128
PAIRS = D // LANES
N = 16
CHUNKS = 3
HALF = D // 2
BF = jnp.bfloat16
F32 = jnp.float32
MESH = pl.DeviceIdType.MESH


def dot(a, b):
    return jnp.dot(a, b, preferred_element_type=F32)


def dot_nt(a, b):
    return lax.dot_general(a, b, (((1,), (1,)), ((), ())), preferred_element_type=F32)


def await_bytes(ref, sem):
    pltpu.make_async_copy(ref, ref, sem).wait()


def transposed(x):
    return jnp.transpose(x.astype(F32)).astype(BF)


def row_dots(ones, grads, outs):
    product = grads.astype(F32) * outs.astype(F32)
    high = product.astype(BF)
    low = (product - high.astype(F32)).astype(BF)
    return dot_nt(ones, high) + dot_nt(ones, low)


def attend(keys, vals, query, grad, keys_t, norm, dots):
    value_parts, key_parts, query_t = [], [], None
    for i in range(2):
        rows = slice(256 * i, 256 * i + 256)
        weights = jnp.exp(dot_nt(keys[rows], query) - norm)
        slopes = dot_nt(vals[rows], grad)
        scores = (weights * (slopes - dots)).astype(BF)
        value_parts.append(dot(weights.astype(BF), grad))
        key_parts.append(dot(scores, query))
        part = dot(keys_t[:, rows], scores)
        query_t = part if query_t is None else query_t + part
    return query_t, jnp.concatenate(key_parts, axis=0), jnp.concatenate(value_parts, axis=0)


def kernel(
    count_ref, moves_ref, q_hbm, k_hbm, v_hbm, o_hbm, norm_hbm, og_hbm, w_hbm, out_ref,
    qv, kv, vv, ov, nv, wv, k_t, tsend, trecv, tabv, tabs,
    ogv, ogf, ogd, sd, gdr, gmf,
    r1a, r1b, r1c, s2, gbuf, em, ebuf, nmsg, nbuf, gm, gdbuf, rsend, rbuf, tmp, acc, xs, total, mix,
    q1a, q1b, q1c, t2, in_sem, p1s, p1r, p1l, p2s, p2r, p2l, o1s, o1r, o1l, o2s, o2r, o2l,
    ss, rs, ls,
):
    me = lax.axis_index("slide")
    seg = lax.axis_index("seg")
    my_z, my_c = me // 2, me % 2
    r1, q1 = (r1a, r1b, r1c), (q1a, q1b, q1c)

    loads = [
        pltpu.make_async_copy(src, dst, in_sem.at[i])
        for i, (src, dst) in enumerate(
            (
                (og_hbm, ogv), (q_hbm, qv), (k_hbm, kv), (v_hbm, vv), (o_hbm, ov),
                (norm_hbm, nv),
            )
        )
    ]
    for k in range(CHUNKS):
        for n in range(3):
            for u in range(2):
                loads.append(
                    pltpu.make_async_copy(
                        w_hbm.at[:, pl.ds(n * D + u * HALF + k * LANES, LANES)],
                        wv.at[k, :, pl.ds((n * 2 + u) * LANES, LANES)],
                        in_sem.at[6],
                    )
                )
    for load in loads:
        load.start()

    barrier = pltpu.get_barrier_semaphore()

    def greet(r, carry):
        pl.semaphore_signal(
            barrier, inc=1, device_id={"slide": lax.rem(me + r, N)}, device_id_type=MESH
        )
        pl.semaphore_signal(
            barrier, inc=1, device_id={"seg": lax.rem(seg + r, N)}, device_id_type=MESH
        )
        return carry

    lax.fori_loop(1, N, greet, 0)

    lane = lax.broadcasted_iota(jnp.int32, (8, LANES), 1)
    sub = lax.broadcasted_iota(jnp.int32, (8, LANES), 0)
    table = jnp.zeros((8, LANES), jnp.int32)
    for t in range(4):
        block = moves_ref[1, t]
        code = jnp.where(block < 4, moves_ref[0, t] * 4 + block, 4 * N)
        table = jnp.where(sub == t, code, table)
        table = jnp.where((sub == 4) & (lane == me * 4 + t), code, table)
    tsend[...] = table
    trecv[pl.ds(me, 1)] = table.reshape(1, 8, LANES)
    for buf in r1 + q1:
        buf[64:68] = jnp.zeros((4, 16, LANES), BF)
    gdr[N] = jnp.zeros((16, HALF), BF)

    pl.semaphore_wait(barrier, 2 * (N - 1))

    def far_first(r):
        step = (r // 2 + 1) // 2
        shift = jnp.where((r // 2) % 2 == 1, 4 - step, 4 + step)
        z = jnp.where(r == 14, my_z, lax.rem(my_z + shift, N // 2))
        return z * 2 + jnp.where(r == 14, 1 - my_c, lax.rem(my_c + r, 2))

    def columns(core, k):
        return pl.ds(pl.multiple_of(core * HALF + k * LANES, LANES), LANES)

    def send_table(r, carry):
        dest = lax.rem(me + r, N)
        pltpu.make_async_remote_copy(
            tsend, trecv.at[me], ss.at[0], rs.at[0], device_id={"slide": dest}, device_id_type=MESH
        ).start()
        return carry

    def spread(k, buf, source, send_sem, recv_sem, local_sem):
        slot = buf.at[pl.ds(me * 4, 4)]

        def one(r, carry):
            dest = far_first(r)
            pltpu.make_async_remote_copy(
                source(dest), slot, send_sem.at[k], recv_sem.at[k],
                device_id={"slide": dest}, device_id_type=MESH,
            ).start()
            return carry

        pltpu.make_async_copy(source(me), slot, local_sem.at[k]).start()
        lax.fori_loop(0, N - 1, one, 0)

    def deliver(k, buf, target, send_sem, recv_sem, local_sem):
        landing = target.at[:, my_z, :, columns(my_c, k)]

        def one(r, carry):
            dest = far_first(r)
            pltpu.make_async_remote_copy(
                buf.at[k, pl.ds(dest * 4, 4)], landing, send_sem.at[k], recv_sem.at[k],
                device_id={"slide": dest}, device_id_type=MESH,
            ).start()
            return carry

        pltpu.make_async_copy(buf.at[k, pl.ds(me * 4, 4)], landing, local_sem.at[k]).start()
        lax.fori_loop(0, N - 1, one, 0)

    def arrived(k, recv_sem, local_sem):
        await_bytes(s2.at[0, pl.ds(0, 60)], recv_sem.at[k])
        await_bytes(s2.at[0, pl.ds(0, 4)], local_sem.at[k])

    def choose(k, row, source, target):
        def one(i, carry):
            target[k, i] = source[tabs[row, i]]
            return carry

        lax.fori_loop(0, 4 * N, one, 0, unroll=8)

    lax.fori_loop(1, N, send_table, 0)
    def spread_in(k):
        spread(k, r1[k], lambda dest: og_hbm.at[:, dest // 2, :, columns(dest % 2, k)], p1s, p1r, p1l)

    spread_in(0)

    first = lax.broadcasted_iota(jnp.int32, (32, LANES), 1) < HS

    def dilate(ref, pair):
        return jnp.where(
            first,
            ref[pl.ds(2 * pair, 32, stride=R), :],
            ref[pl.ds(2 * pair + 1, 32, stride=R), :],
        )

    loads[0].wait()
    for pair in range(PAIRS):
        tmp[pair % 4] = ogv[:, :, :, pair * LANES : (pair + 1) * LANES].reshape(ROWS, LANES).astype(F32)
        picked = dilate(tmp.at[pair % 4], pair)
        up, cols = 8 * (pair // 3), slice((pair % 3) * LANES, (pair % 3 + 1) * LANES)
        for t in range(4):
            ogf[t, up : up + 8, cols] = picked[8 * t : 8 * t + 8]
    ogd[...] = ogf[...].astype(BF)

    def pick_slot(dest, carry):
        slot = jnp.int32(0)
        for t in range(4):
            slot = jnp.where((moves_ref[0, t] == dest) & (moves_ref[1, t] < 4), t, slot)
        sd[dest] = ogd[slot]
        return carry

    lax.fori_loop(0, N, pick_slot, 0)

    def send_dilated(r, carry):
        dest = far_first(r)
        pltpu.make_async_remote_copy(
            sd.at[dest], gdr.at[me], ss.at[5], rs.at[5], device_id={"slide": dest}, device_id_type=MESH
        ).start()
        return carry

    lax.fori_loop(0, N - 1, send_dilated, 0)
    pltpu.make_async_copy(sd.at[me], gdr.at[me], ls.at[5]).start()
    for k in range(1, CHUNKS):
        spread_in(k)

    for load in loads[1:6]:
        load.wait()
    alive = (lax.broadcasted_iota(jnp.int32, (ROWS, LANES), 0) + seg * ROWS) < count_ref[0]
    def prepare(pair, carry):
        cols = pl.ds(pl.multiple_of(pair * LANES, LANES), LANES)
        query = qv[:, cols].astype(F32) * (HS ** -0.5)
        keys = jnp.where(alive, kv[:, cols].astype(F32), 0.0)
        qv[:, cols] = query.astype(BF)
        kv[:, cols] = keys.astype(BF)
        k_t[pair] = jnp.transpose(keys).astype(BF)
        tmp[0] = query
        tmp[1] = keys
        tmp[2] = vv[:, cols].astype(F32)
        tmp[3] = ov[:, cols].astype(F32)
        for n in range(4):
            em[pair, n] = dilate(tmp.at[n], pair).astype(BF)
        return carry

    lax.fori_loop(0, PAIRS, prepare, 0)

    norms = nv[...].reshape(H, ROWS)
    head_row = lax.broadcasted_iota(jnp.int32, (H, ROWS), 0)
    head_lane = lax.broadcasted_iota(jnp.int32, (H, ROWS), 1)
    rest = jnp.where(head_lane % R == head_row, norms, 0.0)
    fold_row = lax.broadcasted_iota(jnp.int32, (ROWS, LANES), 0)
    fold_lane = lax.broadcasted_iota(jnp.int32, (ROWS, LANES), 1)
    fold = jnp.where(fold_row // R + 32 * (seg % 4) == fold_lane, 1.0, 0.0).astype(BF)
    folded = jnp.zeros((H, LANES), F32)
    for _ in range(3):
        piece = rest.astype(BF)
        folded = folded + dot(piece, fold)
        rest = rest - piece.astype(F32)
    for h in range(H):
        nmsg[h] = jnp.broadcast_to(folded[h : h + 1], (8, LANES))

    def send_head(src, dst, index, head):
        @pl.when(head != seg)
        def _():
            pltpu.make_async_remote_copy(
                src, dst, ss.at[index], rs.at[index], device_id={"seg": head}, device_id_type=MESH
            ).start()

        @pl.when(head == seg)
        def _():
            pltpu.make_async_copy(src, dst, ls.at[index]).start()

    def send_early(r, carry):
        head = lax.rem(seg + r, N)

        @pl.when(head < H)
        def _():
            send_head(em.at[head // 2], ebuf.at[seg], 1, head)
            send_head(nmsg.at[head], nbuf.at[seg], 2, head)

        return carry

    lax.fori_loop(0, N, send_early, 0)

    await_bytes(trecv.at[pl.ds(0, N - 1)], rs.at[0])
    inverse = jnp.zeros((8, LANES), jnp.int32)
    codes = jnp.zeros((8, LANES), jnp.int32)
    for d in range(N):
        got = trecv[d]
        inverse = inverse + jnp.where((sub < 4) & (got == lane), d * 4 + sub - 4 * N, 0)
        codes = codes + got
    inverse = jnp.sum(inverse, axis=0, keepdims=True) + 4 * N
    tabv[...] = jnp.clip(jnp.where(sub == 0, inverse, codes), 0, 4 * N)
    table_copy = pltpu.make_async_copy(tabv, tabs, ls.at[0])
    table_copy.start()
    table_copy.wait()

    def relay(k):
        arrived(k, p1r, p1l)
        choose(k, 0, r1[k], s2)
        deliver(k, s2, gbuf, p2s, p2r, p2l)

    relay(0)

    await_bytes(gdr.at[pl.ds(0, N - 1)], rs.at[5])
    await_bytes(gdr.at[0], ls.at[5])
    for b in range(4):
        got = gdr[tabs[0, me * 4 + b] // 4].astype(F32)
        for pair in range(PAIRS):
            up, cols = 8 * (pair // 3), slice((pair % 3) * LANES, (pair % 3 + 1) * LANES)
            gmf[pair, 8 * b : 8 * b + 8, :] = got[up : up + 8, cols]
    sparse_row = lax.broadcasted_iota(jnp.int32, (32, LANES), 0) * R + seg * ROWS
    for pair in range(PAIRS):
        position = sparse_row + jnp.where(first, 2 * pair, 2 * pair + 1)
        gm[pair] = jnp.where(position < count_ref[0], gmf[pair], 0.0).astype(BF)

    def send_grads(r, carry):
        head = lax.rem(seg + r, N)

        @pl.when(head < H)
        def _():
            send_head(gm.at[head // 2], gdbuf.at[seg], 3, head)

        return carry

    lax.fori_loop(0, N, send_grads, 0)

    for k in range(1, CHUNKS):
        relay(k)

    ones_row = lax.broadcasted_iota(jnp.int32, (8, LANES), 0)
    ones_half = lax.broadcasted_iota(jnp.int32, (8, LANES), 1) // HS
    pair_ones = jnp.where(ones_row == ones_half, 1.0, 0.0).astype(BF)
    wide_half = lax.broadcasted_iota(jnp.int32, (ROWS, LANES), 1) // HS

    def sparse_head():
        await_bytes(ebuf.at[pl.ds(0, N - 1)], rs.at[1])
        await_bytes(ebuf.at[0], ls.at[1])
        await_bytes(nbuf.at[pl.ds(0, N - 1)], rs.at[2])
        await_bytes(nbuf.at[0], ls.at[2])
        await_bytes(gdbuf.at[pl.ds(0, N - 1)], rs.at[3])
        await_bytes(gdbuf.at[0], ls.at[3])
        mine = wide_half == seg % 2
        zero = jnp.zeros((ROWS, LANES), BF)
        query = jnp.where(mine, ebuf[:, 0].reshape(ROWS, LANES), zero)
        keys = jnp.where(mine, ebuf[:, 1].reshape(ROWS, LANES), zero)
        vals = ebuf[:, 2].reshape(ROWS, LANES)
        outs = ebuf[:, 3].reshape(ROWS, LANES)
        grad = jnp.where(mine, gdbuf[...].reshape(ROWS, LANES), zero)
        norm = jnp.concatenate(
            [
                sum(nbuf[4 * part + i, 0:1, :] for i in range(4))
                for part in range(4)
            ],
            axis=1,
        )
        dots = row_dots(jnp.ones((8, LANES), BF), grad, outs)[0:1]
        query_t, key_sum, value_sum = attend(
            keys, vals, query, grad, transposed(keys), norm, dots
        )
        rsend[:, 0] = (jnp.transpose(query_t) * (HS ** -0.5)).astype(BF).reshape(N, 32, LANES)
        rsend[:, 1] = key_sum.astype(BF).reshape(N, 32, LANES)
        rsend[:, 2] = value_sum.astype(BF).reshape(N, 32, LANES)

        def back(r, carry):
            dest = lax.rem(seg + r, N)
            pltpu.make_async_remote_copy(
                rsend.at[dest], rbuf.at[seg], ss.at[4], rs.at[4],
                device_id={"seg": dest}, device_id_type=MESH,
            ).start()
            return carry

        lax.fori_loop(1, N, back, 0)
        pltpu.make_async_copy(rsend.at[seg], rbuf.at[seg], ls.at[4]).start()

    @pl.when(seg < H)
    def _():
        sparse_head()

    def chunk(k, carry):
        arrived(k, p2r, p2l)

        def local_pair(u, inner):
            pair = u * CHUNKS + k
            cols = pl.ds(pl.multiple_of(pair * LANES, LANES), LANES)
            query, keys, vals = qv[:, cols], kv[:, cols], vv[:, cols]
            grad = jnp.where(
                alive, gbuf[:, :, :, cols].reshape(ROWS, LANES).astype(F32), 0.0
            ).astype(BF)
            zero = jnp.zeros((ROWS, LANES), BF)
            dots = row_dots(pair_ones, grad, ov[:, cols])
            query_parts, key_sum, value_sum = [], None, None
            for x in range(2):
                mine = wide_half == x
                query_t, key_part, value_part = attend(
                    keys, vals, jnp.where(mine, query, zero), jnp.where(mine, grad, zero),
                    k_t[pair, x * HS : (x + 1) * HS, :],
                    nv[2 * pair + x], dots[x : x + 1],
                )
                query_parts.append(query_t)
                key_sum = key_part if key_sum is None else key_sum + key_part
                value_sum = value_part if value_sum is None else value_sum + value_part
            acc[0] = jnp.transpose(jnp.concatenate(query_parts, axis=0)) * (HS ** -0.5)
            acc[1] = key_sum
            acc[2] = value_sum

            @pl.when((u == 0) & (k == 0) & (seg < H))
            def _():
                await_bytes(rbuf.at[pl.ds(0, H - 1)], rs.at[4])
                await_bytes(rbuf.at[0], ls.at[4])

            @pl.when((u == 0) & (k == 0) & (seg >= H))
            def _():
                await_bytes(rbuf, rs.at[4])

            for n in range(3):
                place = acc.at[n]
                for x in range(2):
                    rows = pl.ds(2 * pair + x, 32, stride=R)
                    place[rows, :] = place[rows, :] + rbuf[2 * pair + x, n].astype(F32)
                where = pl.ds(pl.multiple_of((n * 2 + u) * LANES, LANES), LANES)
                xs[:, where] = place[...].astype(BF)
            return inner

        lax.fori_loop(0, 2, local_pair, 0)

        @pl.when(k == 0)
        def _():
            for load in loads[6:]:
                load.wait()
            total[...] = dot_nt(xs[...], wv[0])

        @pl.when(k == 1)
        def _():
            total[...] += dot_nt(xs[...], wv[1])

        return carry

    lax.fori_loop(0, CHUNKS, chunk, 0)

    for k in range(CHUNKS):
        for core in range(2):
            cols = slice(core * HALF + k * LANES, core * HALF + (k + 1) * LANES)
            mixed = total[:, cols] + dot_nt(xs[...], wv[CHUNKS - 1, cols, :])
            mix[k, core] = jnp.where(alive, mixed, 0.0).astype(BF).reshape(4, 8, 16, LANES)
        spread(
            k, q1[k], lambda dest, k=k: mix.at[k, dest % 2, :, dest // 2], o1s, o1r, o1l
        )

    for k in range(CHUNKS):
        arrived(k, o1r, o1l)
        choose(k, 4, q1[k], t2)
        deliver(k, t2, out_ref, o2s, o2r, o2l)
    for k in range(CHUNKS):
        arrived(k, o2r, o2l)

    for sems in (p1s, p2s, o1s, o2s):
        for k in range(CHUNKS):
            await_bytes(s2.at[0, pl.ds(0, 60)], sems.at[k])
    await_bytes(trecv.at[pl.ds(0, N - 1)], ss.at[0])
    await_bytes(gdr.at[pl.ds(0, N - 1)], ss.at[5])

    @pl.when(seg < H)
    def _():
        await_bytes(ebuf.at[pl.ds(0, H - 1)], ss.at[1])
        await_bytes(nbuf.at[pl.ds(0, H - 1)], ss.at[2])
        await_bytes(gdbuf.at[pl.ds(0, H - 1)], ss.at[3])
        await_bytes(rsend.at[pl.ds(0, N - 1)], ss.at[4])

    @pl.when(seg >= H)
    def _():
        await_bytes(ebuf.at[pl.ds(0, H)], ss.at[1])
        await_bytes(nbuf.at[pl.ds(0, H)], ss.at[2])
        await_bytes(gdbuf.at[pl.ds(0, H)], ss.at[3])


def shards(counts, moves, queries, key_rows, values, forward_out, log_norms, out_grads, weights):
    dma = pltpu.SemaphoreType.DMA
    vmem = pltpu.VMEM
    hbm_spec = pl.BlockSpec(memory_space=pltpu.HBM)
    smem_spec = pl.BlockSpec(memory_space=pltpu.SMEM)
    scratch = [
        *[vmem((ROWS, D), BF)] * 4,
        vmem((H, 1, ROWS), F32),
        vmem((CHUNKS, D, D), BF),
        vmem((PAIRS, LANES, ROWS), BF),
        vmem((8, LANES), jnp.int32),
        vmem((N, 8, LANES), jnp.int32),
        vmem((8, LANES), jnp.int32),
        pltpu.SMEM((8, LANES), jnp.int32),
        vmem((4, 8, 16, D), BF),
        vmem((4, 16, HALF), F32),
        vmem((4, 16, HALF), BF),
        vmem((N, 16, HALF), BF),
        vmem((N + 1, 16, HALF), BF),
        vmem((PAIRS, 32, LANES), F32),
        *[vmem((68, 16, LANES), BF)] * 3,
        vmem((CHUNKS, 64, 16, LANES), BF),
        vmem((4, 8, 16, D), BF),
        vmem((PAIRS, 4, 32, LANES), BF),
        vmem((N, 4, 32, LANES), BF),
        vmem((H, 8, LANES), F32),
        vmem((N, 8, LANES), F32),
        vmem((PAIRS, 32, LANES), BF),
        vmem((N, 32, LANES), BF),
        vmem((N, 3, 32, LANES), BF),
        vmem((H, 3, 32, LANES), BF),
        vmem((4, ROWS, LANES), F32),
        vmem((3, ROWS, LANES), F32),
        vmem((ROWS, D), BF),
        vmem((ROWS, D), F32),
        vmem((CHUNKS, 2, 4, 8, 16, LANES), BF),
        *[vmem((68, 16, LANES), BF)] * 3,
        vmem((CHUNKS, 64, 16, LANES), BF),
        dma((7,)),
        *[dma((CHUNKS,))] * 12,
        *[dma((6,))] * 3,
    ]
    result = pl.pallas_call(
        kernel,
        out_shape=jax.ShapeDtypeStruct((4, 8, 16, D), BF),
        in_specs=[smem_spec, smem_spec] + [hbm_spec] * 7,
        out_specs=hbm_spec,
        scratch_shapes=scratch,
        compiler_params=pltpu.CompilerParams(
            collective_id=0, has_side_effects=True, vmem_limit_bytes=56 * 1024 * 1024
        ),
        name="dilated_backward",
    )(
        counts,
        moves[0, 0],
        queries[0],
        key_rows[0],
        values[0],
        forward_out[0],
        jnp.transpose(log_norms, (1, 0, 2)),
        out_grads[0].reshape(4, 8, 16, D),
        weights,
    )
    return result.reshape(1, ROWS, D)


def solution(mesh):
    return jax.shard_map(
        shards,
        mesh=mesh,
        in_specs=(
            P("slide"),
            P("slide", "seg", None, None),
            P("slide", "seg", None),
            P("slide", "seg", None),
            P("slide", "seg", None),
            P("slide", "seg", None),
            P("slide", None, "seg"),
            P("slide", "seg", None),
            P(),
        ),
        out_specs=P("slide", "seg", None),
        check_vma=False,
    )
```

```python
import jax
import jax.numpy as jnp
from jax import lax
from jax.experimental import pallas as pl
from jax.experimental.pallas import tpu as pltpu
from jax.sharding import PartitionSpec as P

D = 768
H = 12
R = 16
BLK = 128
ROWS = 512
HS = D // H
LANES = 128
PAIRS = D // LANES
N = 16
CHUNKS = 3
HALF = D // 2
BF = jnp.bfloat16
F32 = jnp.float32
MESH = pl.DeviceIdType.MESH


def dot(a, b):
    return jnp.dot(a, b, preferred_element_type=F32)


def dot_nt(a, b):
    return lax.dot_general(a, b, (((1,), (1,)), ((), ())), preferred_element_type=F32)


def await_bytes(ref, sem):
    pltpu.make_async_copy(ref, ref, sem).wait()


def transposed(x):
    return jnp.transpose(x.astype(F32)).astype(BF)


def row_dots(ones, grads, outs):
    product = grads.astype(F32) * outs.astype(F32)
    high = product.astype(BF)
    low = (product - high.astype(F32)).astype(BF)
    return dot_nt(ones, high) + dot_nt(ones, low)


def weigh(keys, query, norm):
    return jnp.exp(dot_nt(keys, query) - norm)


def attend(weights_of, keys_t, vals, query, grad, dots):
    value_parts, key_parts, query_t = [], [], None
    for i in range(2):
        rows = slice(256 * i, 256 * i + 256)
        weights = weights_of(rows)
        slopes = dot_nt(vals[rows], grad)
        scores = (weights * (slopes - dots)).astype(BF)
        value_parts.append(dot(weights.astype(BF), grad))
        key_parts.append(dot(scores, query))
        part = dot(keys_t[:, rows], scores)
        query_t = part if query_t is None else query_t + part
    return query_t, jnp.concatenate(key_parts, axis=0), jnp.concatenate(value_parts, axis=0)


def kernel(
    count_ref, moves_ref, q_hbm, k_hbm, v_hbm, o_hbm, norm_hbm, og_hbm, w_hbm, out_ref,
    qv, kv, vv, ov, nv, wv, k_t, tsend, trecv, tabv, tabs,
    ogv, ogf, ogd, sd, gdr, gmf,
    r1a, r1b, r1c, s2, gbuf, em, ebuf, nmsg, nbuf, gm, gdbuf, rsend, rbuf, held, tmp, acc, xs, total, mix,
    q1a, q1b, q1c, t2, in_sem, p1s, p1r, p1l, p2s, p2r, p2l, o1s, o1r, o1l, o2s, o2r, o2l,
    ss, rs, ls,
):
    me = lax.axis_index("slide")
    seg = lax.axis_index("seg")
    my_z, my_c = me // 2, me % 2
    r1, q1 = (r1a, r1b, r1c), (q1a, q1b, q1c)

    barrier = pltpu.get_barrier_semaphore()

    def greet(r, carry):
        pl.semaphore_signal(
            barrier, inc=1, device_id={"slide": lax.rem(me + r, N)}, device_id_type=MESH
        )
        pl.semaphore_signal(
            barrier, inc=1, device_id={"seg": lax.rem(seg + r, N)}, device_id_type=MESH
        )
        return carry

    lax.fori_loop(1, N, greet, 0)

    loads = [
        pltpu.make_async_copy(src, dst, in_sem.at[i])
        for i, (src, dst) in enumerate(
            (
                (og_hbm, ogv), (q_hbm, qv), (k_hbm, kv), (v_hbm, vv), (o_hbm, ov),
                (norm_hbm, nv),
            )
        )
    ]
    for k in range(CHUNKS):
        for n in range(3):
            for u in range(2):
                loads.append(
                    pltpu.make_async_copy(
                        w_hbm.at[:, pl.ds(n * D + u * HALF + k * LANES, LANES)],
                        wv.at[k, :, pl.ds((n * 2 + u) * LANES, LANES)],
                        in_sem.at[6],
                    )
                )
    for load in loads[:6]:
        load.start()

    lane = lax.broadcasted_iota(jnp.int32, (1, LANES), 1)
    table = jnp.zeros((1, LANES), jnp.int32)
    for t in range(4):
        block = moves_ref[1, t]
        code = jnp.where(block < 4, moves_ref[0, t] * 4 + block, 4 * N)
        table = jnp.where(lane == me * 4 + t, code, table)
    tsend[...] = table
    trecv[me] = table
    for buf in r1 + q1:
        buf[64:68] = jnp.zeros((4, 16, LANES), BF)
    gdr[N] = jnp.zeros((16, HALF), BF)

    pl.semaphore_wait(barrier, 2 * (N - 1))

    def far_first(r):
        step = (r // 2 + 1) // 2
        shift = jnp.where((r // 2) % 2 == 1, 4 - step, 4 + step)
        z = jnp.where(r == 14, my_z, lax.rem(my_z + shift, N // 2))
        return z * 2 + jnp.where(r == 14, 1 - my_c, lax.rem(my_c + r, 2))

    def columns(core, k):
        return pl.ds(pl.multiple_of(core * HALF + k * LANES, LANES), LANES)

    def send_table(r, carry):
        dest = lax.rem(me + r, N)
        pltpu.make_async_remote_copy(
            tsend, trecv.at[me], ss.at[0], rs.at[0], device_id={"slide": dest}, device_id_type=MESH
        ).start()
        return carry

    def spread(k, buf, source, send_sem, recv_sem, local_sem):
        slot = buf.at[pl.ds(me * 4, 4)]

        def one(r, carry):
            dest = far_first(r)
            pltpu.make_async_remote_copy(
                source(dest), slot, send_sem.at[k], recv_sem.at[k],
                device_id={"slide": dest}, device_id_type=MESH,
            ).start()
            return carry

        pltpu.make_async_copy(source(me), slot, local_sem.at[k]).start()
        lax.fori_loop(0, N - 1, one, 0)

    def deliver(k, buf, target, send_sem, recv_sem, local_sem):
        landing = target.at[:, my_z, :, columns(my_c, k)]

        def one(r, carry):
            dest = far_first(r)
            pltpu.make_async_remote_copy(
                buf.at[k, pl.ds(dest * 4, 4)], landing, send_sem.at[k], recv_sem.at[k],
                device_id={"slide": dest}, device_id_type=MESH,
            ).start()
            return carry

        pltpu.make_async_copy(buf.at[k, pl.ds(me * 4, 4)], landing, local_sem.at[k]).start()
        lax.fori_loop(0, N - 1, one, 0)

    def arrived(k, recv_sem, local_sem):
        await_bytes(s2.at[0, pl.ds(0, 60)], recv_sem.at[k])
        await_bytes(s2.at[0, pl.ds(0, 4)], local_sem.at[k])

    def choose(k, row, source, target):
        def one(i, carry):
            target[k, i] = source[tabs[row, i]]
            return carry

        lax.fori_loop(0, 4 * N, one, 0, unroll=8)

    lax.fori_loop(1, N, send_table, 0)
    def spread_in(k):
        spread(k, r1[k], lambda dest: og_hbm.at[:, dest // 2, :, columns(dest % 2, k)], p1s, p1r, p1l)

    spread_in(0)

    first = lax.broadcasted_iota(jnp.int32, (32, LANES), 1) < HS

    def dilate(ref, pair):
        return jnp.where(
            first,
            ref[pl.ds(2 * pair, 32, stride=R), :],
            ref[pl.ds(2 * pair + 1, 32, stride=R), :],
        )

    loads[0].wait()
    for pair in range(PAIRS):
        tmp[pair % 4] = ogv[:, :, :, pair * LANES : (pair + 1) * LANES].reshape(ROWS, LANES).astype(F32)
        picked = dilate(tmp.at[pair % 4], pair)
        up, cols = 8 * (pair // 3), slice((pair % 3) * LANES, (pair % 3 + 1) * LANES)
        for t in range(4):
            ogf[t, up : up + 8, cols] = picked[8 * t : 8 * t + 8]
    ogd[...] = ogf[...].astype(BF)

    def pick_slot(dest, carry):
        slot = jnp.int32(0)
        for t in range(4):
            slot = jnp.where((moves_ref[0, t] == dest) & (moves_ref[1, t] < 4), t, slot)
        sd[dest] = ogd[slot]
        return carry

    lax.fori_loop(0, N, pick_slot, 0)

    def send_dilated(r, carry):
        dest = far_first(r)
        pltpu.make_async_remote_copy(
            sd.at[dest], gdr.at[me], ss.at[5], rs.at[5], device_id={"slide": dest}, device_id_type=MESH
        ).start()
        return carry

    lax.fori_loop(0, N - 1, send_dilated, 0)
    pltpu.make_async_copy(sd.at[me], gdr.at[me], ls.at[5]).start()
    for k in range(1, CHUNKS):
        spread_in(k)
    for load in loads[6:]:
        load.start()

    for load in loads[1:6]:
        load.wait()
    alive = (lax.broadcasted_iota(jnp.int32, (ROWS, LANES), 0) + seg * ROWS) < count_ref[0]
    def prepare(pair, carry):
        cols = pl.ds(pl.multiple_of(pair * LANES, LANES), LANES)
        query = qv[:, cols].astype(F32) * (HS ** -0.5)
        keys = jnp.where(alive, kv[:, cols].astype(F32), 0.0)
        qv[:, cols] = query.astype(BF)
        kv[:, cols] = keys.astype(BF)
        k_t[pair] = jnp.transpose(keys).astype(BF)
        tmp[0] = query
        tmp[1] = keys
        tmp[2] = vv[:, cols].astype(F32)
        tmp[3] = ov[:, cols].astype(F32)
        for n in range(4):
            em[pair, n] = dilate(tmp.at[n], pair).astype(BF)
        return carry

    lax.fori_loop(0, PAIRS, prepare, 0)

    norms = nv[...].reshape(H, ROWS)
    head_row = lax.broadcasted_iota(jnp.int32, (H, ROWS), 0)
    head_lane = lax.broadcasted_iota(jnp.int32, (H, ROWS), 1)
    rest = jnp.where(head_lane % R == head_row, norms, 0.0)
    fold_row = lax.broadcasted_iota(jnp.int32, (ROWS, LANES), 0)
    fold_lane = lax.broadcasted_iota(jnp.int32, (ROWS, LANES), 1)
    fold = jnp.where(fold_row // R + 32 * (seg % 4) == fold_lane, 1.0, 0.0).astype(BF)
    folded = jnp.zeros((H, LANES), F32)
    for _ in range(3):
        piece = rest.astype(BF)
        folded = folded + dot(piece, fold)
        rest = rest - piece.astype(F32)
    for h in range(H):
        nmsg[h] = jnp.broadcast_to(folded[h : h + 1], (8, LANES))

    def send_head(src, dst, index, head):
        @pl.when(head != seg)
        def _():
            pltpu.make_async_remote_copy(
                src, dst, ss.at[index], rs.at[index], device_id={"seg": head}, device_id_type=MESH
            ).start()

        @pl.when(head == seg)
        def _():
            pltpu.make_async_copy(src, dst, ls.at[index]).start()

    def send_early(r, carry):
        head = lax.rem(seg + r, N)

        @pl.when(head < H)
        def _():
            send_head(em.at[head // 2], ebuf.at[seg], 1, head)
            send_head(nmsg.at[head], nbuf.at[seg], 2, head)

        return carry

    lax.fori_loop(0, N, send_early, 0)

    await_bytes(trecv.at[pl.ds(0, N - 1)], rs.at[0])
    codes = jnp.zeros((1, LANES), jnp.int32)
    for d in range(N):
        codes = codes + trecv[d]
    down = jnp.transpose(jnp.broadcast_to(codes.astype(F32), (LANES, LANES)))
    spot = lax.broadcasted_iota(jnp.int32, (LANES, LANES), 0)
    match = (down.astype(jnp.int32) == lax.broadcasted_iota(jnp.int32, (LANES, LANES), 1)) & (spot < 4 * N)
    inverse = jnp.sum(jnp.where(match, spot - 4 * N, 0), axis=0, keepdims=True) + 4 * N
    sub = lax.broadcasted_iota(jnp.int32, (8, LANES), 0)
    tabv[...] = jnp.clip(
        jnp.where(
            sub == 0, jnp.broadcast_to(inverse, (8, LANES)), jnp.broadcast_to(codes, (8, LANES))
        ),
        0,
        4 * N,
    )
    table_copy = pltpu.make_async_copy(tabv, tabs, ls.at[0])
    table_copy.start()
    table_copy.wait()

    def relay(k):
        arrived(k, p1r, p1l)
        choose(k, 0, r1[k], s2)
        deliver(k, s2, gbuf, p2s, p2r, p2l)

    relay(0)

    await_bytes(gdr.at[pl.ds(0, N - 1)], rs.at[5])
    await_bytes(gdr.at[0], ls.at[5])
    for b in range(4):
        got = gdr[tabs[0, me * 4 + b] // 4].astype(F32)
        for pair in range(PAIRS):
            up, cols = 8 * (pair // 3), slice((pair % 3) * LANES, (pair % 3 + 1) * LANES)
            gmf[pair, 8 * b : 8 * b + 8, :] = got[up : up + 8, cols]
    sparse_row = lax.broadcasted_iota(jnp.int32, (32, LANES), 0) * R + seg * ROWS
    for pair in range(PAIRS):
        position = sparse_row + jnp.where(first, 2 * pair, 2 * pair + 1)
        gm[pair] = jnp.where(position < count_ref[0], gmf[pair], 0.0).astype(BF)

    def send_grads(r, carry):
        head = lax.rem(seg + r, N)

        @pl.when(head < H)
        def _():
            send_head(gm.at[head // 2], gdbuf.at[seg], 3, head)

        return carry

    lax.fori_loop(0, N, send_grads, 0)

    wide_half = lax.broadcasted_iota(jnp.int32, (ROWS, LANES), 1) // HS

    def local_weights(k):
        def one(u, carry):
            pair = u * CHUNKS + k
            cols = pl.ds(pl.multiple_of(pair * LANES, LANES), LANES)
            query = qv[:, cols]
            for x in range(2):
                masked = jnp.where(wide_half == x, query, jnp.zeros((ROWS, LANES), BF))
                for i in range(2):
                    rows = slice(256 * i, 256 * i + 256)
                    held[2 * pair + x, rows, :] = weigh(kv[rows, cols], masked, nv[2 * pair + x])
            return carry

        lax.fori_loop(0, 2, one, 0)

    for k in range(1, CHUNKS):
        local_weights(k - 1)
        relay(k)

    ones_row = lax.broadcasted_iota(jnp.int32, (8, LANES), 0)
    ones_half = lax.broadcasted_iota(jnp.int32, (8, LANES), 1) // HS
    pair_ones = jnp.where(ones_row == ones_half, 1.0, 0.0).astype(BF)

    def sparse_head():
        await_bytes(ebuf.at[pl.ds(0, N - 1)], rs.at[1])
        await_bytes(ebuf.at[0], ls.at[1])
        await_bytes(nbuf.at[pl.ds(0, N - 1)], rs.at[2])
        await_bytes(nbuf.at[0], ls.at[2])
        await_bytes(gdbuf.at[pl.ds(0, N - 1)], rs.at[3])
        await_bytes(gdbuf.at[0], ls.at[3])
        mine = wide_half == seg % 2
        zero = jnp.zeros((ROWS, LANES), BF)
        query = jnp.where(mine, ebuf[:, 0].reshape(ROWS, LANES), zero)
        keys = jnp.where(mine, ebuf[:, 1].reshape(ROWS, LANES), zero)
        vals = ebuf[:, 2].reshape(ROWS, LANES)
        outs = ebuf[:, 3].reshape(ROWS, LANES)
        grad = jnp.where(mine, gdbuf[...].reshape(ROWS, LANES), zero)
        norm = jnp.concatenate(
            [
                sum(nbuf[4 * part + i, 0:1, :] for i in range(4))
                for part in range(4)
            ],
            axis=1,
        )
        dots = row_dots(jnp.ones((8, LANES), BF), grad, outs)[0:1]
        query_t, key_sum, value_sum = attend(
            lambda rows: weigh(keys[rows], query, norm), transposed(keys), vals, query, grad, dots
        )
        rsend[:, 0] = (jnp.transpose(query_t) * (HS ** -0.5)).astype(BF).reshape(N, 32, LANES)
        rsend[:, 1] = key_sum.astype(BF).reshape(N, 32, LANES)
        rsend[:, 2] = value_sum.astype(BF).reshape(N, 32, LANES)

        def back(r, carry):
            dest = lax.rem(seg + r, N)
            pltpu.make_async_remote_copy(
                rsend.at[dest], rbuf.at[seg], ss.at[4], rs.at[4],
                device_id={"seg": dest}, device_id_type=MESH,
            ).start()
            return carry

        lax.fori_loop(1, N, back, 0)
        pltpu.make_async_copy(rsend.at[seg], rbuf.at[seg], ls.at[4]).start()

    @pl.when(seg < H)
    def _():
        sparse_head()

    local_weights(CHUNKS - 1)

    def chunk(k, carry):
        arrived(k, p2r, p2l)

        def local_pair(u, inner):
            pair = u * CHUNKS + k
            cols = pl.ds(pl.multiple_of(pair * LANES, LANES), LANES)
            query, vals = qv[:, cols], vv[:, cols]
            grad = jnp.where(
                alive, gbuf[:, :, :, cols].reshape(ROWS, LANES).astype(F32), 0.0
            ).astype(BF)
            zero = jnp.zeros((ROWS, LANES), BF)
            dots = row_dots(pair_ones, grad, ov[:, cols])
            query_parts, key_sum, value_sum = [], None, None
            for x in range(2):
                mine = wide_half == x
                query_t, key_part, value_part = attend(
                    lambda rows, x=x: held[2 * pair + x, rows, :], k_t[pair, x * HS : (x + 1) * HS, :],
                    vals, jnp.where(mine, query, zero), jnp.where(mine, grad, zero), dots[x : x + 1],
                )
                query_parts.append(query_t)
                key_sum = key_part if key_sum is None else key_sum + key_part
                value_sum = value_part if value_sum is None else value_sum + value_part
            acc[0] = jnp.transpose(jnp.concatenate(query_parts, axis=0)) * (HS ** -0.5)
            acc[1] = key_sum
            acc[2] = value_sum

            @pl.when((u == 0) & (k == 0) & (seg < H))
            def _():
                await_bytes(rbuf.at[pl.ds(0, H - 1)], rs.at[4])
                await_bytes(rbuf.at[0], ls.at[4])

            @pl.when((u == 0) & (k == 0) & (seg >= H))
            def _():
                await_bytes(rbuf, rs.at[4])

            for n in range(3):
                place = acc.at[n]
                for x in range(2):
                    rows = pl.ds(2 * pair + x, 32, stride=R)
                    place[rows, :] = place[rows, :] + rbuf[2 * pair + x, n].astype(F32)
                where = pl.ds(pl.multiple_of((n * 2 + u) * LANES, LANES), LANES)
                xs[:, where] = place[...].astype(BF)
            return inner

        lax.fori_loop(0, 2, local_pair, 0)

        @pl.when(k == 0)
        def _():
            for load in loads[6:]:
                load.wait()
            total[...] = dot_nt(xs[...], wv[0])

        @pl.when(k == 1)
        def _():
            total[...] += dot_nt(xs[...], wv[1])

        return carry

    lax.fori_loop(0, CHUNKS, chunk, 0)

    for k in range(CHUNKS):
        for core in range(2):
            cols = slice(core * HALF + k * LANES, core * HALF + (k + 1) * LANES)
            mixed = total[:, cols] + dot_nt(xs[...], wv[CHUNKS - 1, cols, :])
            mix[k, core] = jnp.where(alive, mixed, 0.0).astype(BF).reshape(4, 8, 16, LANES)
        spread(
            k, q1[k], lambda dest, k=k: mix.at[k, dest % 2, :, dest // 2], o1s, o1r, o1l
        )

    for k in range(CHUNKS):
        arrived(k, o1r, o1l)
        choose(k, 4, q1[k], t2)
        deliver(k, t2, out_ref, o2s, o2r, o2l)
    for k in range(CHUNKS):
        arrived(k, o2r, o2l)

    for sems in (p1s, p2s, o1s, o2s):
        for k in range(CHUNKS):
            await_bytes(s2.at[0, pl.ds(0, 60)], sems.at[k])
    await_bytes(trecv.at[pl.ds(0, N - 1)], ss.at[0])
    await_bytes(gdr.at[pl.ds(0, N - 1)], ss.at[5])

    @pl.when(seg < H)
    def _():
        await_bytes(ebuf.at[pl.ds(0, H - 1)], ss.at[1])
        await_bytes(nbuf.at[pl.ds(0, H - 1)], ss.at[2])
        await_bytes(gdbuf.at[pl.ds(0, H - 1)], ss.at[3])
        await_bytes(rsend.at[pl.ds(0, N - 1)], ss.at[4])

    @pl.when(seg >= H)
    def _():
        await_bytes(ebuf.at[pl.ds(0, H)], ss.at[1])
        await_bytes(nbuf.at[pl.ds(0, H)], ss.at[2])
        await_bytes(gdbuf.at[pl.ds(0, H)], ss.at[3])


def shards(counts, moves, queries, key_rows, values, forward_out, log_norms, out_grads, weights):
    dma = pltpu.SemaphoreType.DMA
    vmem = pltpu.VMEM
    hbm_spec = pl.BlockSpec(memory_space=pltpu.HBM)
    smem_spec = pl.BlockSpec(memory_space=pltpu.SMEM)
    scratch = [
        *[vmem((ROWS, D), BF)] * 4,
        vmem((H, 1, ROWS), F32),
        vmem((CHUNKS, D, D), BF),
        vmem((PAIRS, LANES, ROWS), BF),
        vmem((1, LANES), jnp.int32),
        vmem((N, 1, LANES), jnp.int32),
        vmem((8, LANES), jnp.int32),
        pltpu.SMEM((8, LANES), jnp.int32),
        vmem((4, 8, 16, D), BF),
        vmem((4, 16, HALF), F32),
        vmem((4, 16, HALF), BF),
        vmem((N, 16, HALF), BF),
        vmem((N + 1, 16, HALF), BF),
        vmem((PAIRS, 32, LANES), F32),
        *[vmem((68, 16, LANES), BF)] * 3,
        vmem((CHUNKS, 64, 16, LANES), BF),
        vmem((4, 8, 16, D), BF),
        vmem((PAIRS, 4, 32, LANES), BF),
        vmem((N, 4, 32, LANES), BF),
        vmem((H, 8, LANES), F32),
        vmem((N, 8, LANES), F32),
        vmem((PAIRS, 32, LANES), BF),
        vmem((N, 32, LANES), BF),
        vmem((N, 3, 32, LANES), BF),
        vmem((H, 3, 32, LANES), BF),
        vmem((H, ROWS, ROWS), F32),
        vmem((4, ROWS, LANES), F32),
        vmem((3, ROWS, LANES), F32),
        vmem((ROWS, D), BF),
        vmem((ROWS, D), F32),
        vmem((CHUNKS, 2, 4, 8, 16, LANES), BF),
        *[vmem((68, 16, LANES), BF)] * 3,
        vmem((CHUNKS, 64, 16, LANES), BF),
        dma((7,)),
        *[dma((CHUNKS,))] * 12,
        *[dma((6,))] * 3,
    ]
    result = pl.pallas_call(
        kernel,
        out_shape=jax.ShapeDtypeStruct((4, 8, 16, D), BF),
        in_specs=[smem_spec, smem_spec] + [hbm_spec] * 7,
        out_specs=hbm_spec,
        scratch_shapes=scratch,
        compiler_params=pltpu.CompilerParams(
            collective_id=0, has_side_effects=True, vmem_limit_bytes=56 * 1024 * 1024
        ),
        name="dilated_backward",
    )(
        counts,
        moves[0, 0],
        queries[0],
        key_rows[0],
        values[0],
        forward_out[0],
        jnp.transpose(log_norms, (1, 0, 2)),
        out_grads[0].reshape(4, 8, 16, D),
        weights,
    )
    return result.reshape(1, ROWS, D)


def solution(mesh):
    return jax.shard_map(
        shards,
        mesh=mesh,
        in_specs=(
            P("slide"),
            P("slide", "seg", None, None),
            P("slide", "seg", None),
            P("slide", "seg", None),
            P("slide", "seg", None),
            P("slide", "seg", None),
            P("slide", None, "seg"),
            P("slide", "seg", None),
            P(),
        ),
        out_specs=P("slide", "seg", None),
        check_vma=False,
    )
```

```python
import jax
import jax.numpy as jnp
from jax import lax
from jax.experimental import pallas as pl
from jax.experimental.pallas import tpu as pltpu
from jax.sharding import PartitionSpec as P

D = 768
H = 12
R = 16
BLK = 128
ROWS = 512
HS = D // H
LANES = 128
PAIRS = D // LANES
N = 16
CHUNKS = 3
HALF = D // 2
AHEAD = (1, 2, 4, 5)
AHEAD_COLS = 2 * LANES
BF = jnp.bfloat16
F32 = jnp.float32
MESH = pl.DeviceIdType.MESH


def dot(a, b):
    return jnp.dot(a, b, preferred_element_type=F32)


def dot_nt(a, b):
    return lax.dot_general(a, b, (((1,), (1,)), ((), ())), preferred_element_type=F32)


def await_bytes(ref, sem):
    pltpu.make_async_copy(ref, ref, sem).wait()


def transposed(x):
    return jnp.transpose(x.astype(F32)).astype(BF)


def row_dots(ones, grads, outs):
    product = grads.astype(F32) * outs.astype(F32)
    high = product.astype(BF)
    low = (product - high.astype(F32)).astype(BF)
    return dot_nt(ones, high) + dot_nt(ones, low)


def weigh(keys, query, norm):
    return jnp.exp(dot_nt(keys, query) - norm)


def attend(weights_of, keys_t, vals, query, grad, dots):
    value_parts, key_parts, query_t = [], [], None
    for i in range(2):
        rows = slice(256 * i, 256 * i + 256)
        weights = weights_of(rows)
        slopes = dot_nt(vals[rows], grad)
        scores = (weights * (slopes - dots)).astype(BF)
        value_parts.append(dot(weights.astype(BF), grad))
        key_parts.append(dot(scores, query))
        part = dot(keys_t[:, rows], scores)
        query_t = part if query_t is None else query_t + part
    return query_t, jnp.concatenate(key_parts, axis=0), jnp.concatenate(value_parts, axis=0)


def kernel(
    count_ref, moves_ref, q_hbm, k_hbm, v_hbm, o_hbm, norm_hbm, og_hbm, w_hbm, out_ref,
    qv, kv, vv, ov, nv, wv, k_t, tsend, trecv, tabv, tabs,
    ogv, ogf, ogd, sd, gdr, gmf,
    r1a, r1b, r1c, s2, gbuf, em, ebuf, nmsg, nbuf, gm, gdbuf, rsend, rbuf, held, tmp, acc, xs, total, mix,
    q1a, q1b, q1c, t2, in_sem, p1s, p1r, p1l, p2s, p2r, p2l, o1s, o1r, o1l, o2s, o2r, o2l,
    ss, rs, ls,
):
    me = lax.axis_index("slide")
    seg = lax.axis_index("seg")
    my_z, my_c = me // 2, me % 2
    r1, q1 = (r1a, r1b, r1c), (q1a, q1b, q1c)

    barrier = pltpu.get_barrier_semaphore()

    def greet(r, carry):
        pl.semaphore_signal(
            barrier, inc=1, device_id={"slide": lax.rem(me + r, N)}, device_id_type=MESH
        )
        pl.semaphore_signal(
            barrier, inc=1, device_id={"seg": lax.rem(seg + r, N)}, device_id_type=MESH
        )
        return carry

    lax.fori_loop(1, N, greet, 0)

    loads = [
        pltpu.make_async_copy(src, dst, in_sem.at[i])
        for i, (src, dst) in enumerate(
            (
                (og_hbm, ogv), (q_hbm, qv), (k_hbm, kv), (v_hbm, vv), (o_hbm, ov),
                (norm_hbm, nv),
            )
        )
    ]
    for k in range(CHUNKS):
        for n in range(3):
            for u in range(2):
                loads.append(
                    pltpu.make_async_copy(
                        w_hbm.at[:, pl.ds(n * D + u * HALF + k * LANES, LANES)],
                        wv.at[k, :, pl.ds((n * 2 + u) * LANES, LANES)],
                        in_sem.at[6],
                    )
                )
    for load in loads[:6]:
        load.start()

    lane = lax.broadcasted_iota(jnp.int32, (1, LANES), 1)
    table = jnp.zeros((1, LANES), jnp.int32)
    for t in range(4):
        block = moves_ref[1, t]
        code = jnp.where(block < 4, moves_ref[0, t] * 4 + block, 4 * N)
        table = jnp.where(lane == me * 4 + t, code, table)
    tsend[...] = table
    trecv[me] = table
    for buf in r1 + q1:
        buf[64:68] = jnp.zeros((4, 16, LANES), BF)
    gdr[N] = jnp.zeros((16, AHEAD_COLS), BF)

    pl.semaphore_wait(barrier, 2 * (N - 1))

    def far_first(r):
        step = (r // 2 + 1) // 2
        shift = jnp.where((r // 2) % 2 == 1, 4 - step, 4 + step)
        z = jnp.where(r == 14, my_z, lax.rem(my_z + shift, N // 2))
        return z * 2 + jnp.where(r == 14, 1 - my_c, lax.rem(my_c + r, 2))

    def columns(core, k):
        return pl.ds(pl.multiple_of(core * HALF + k * LANES, LANES), LANES)

    def send_table(r, carry):
        dest = lax.rem(me + r, N)
        pltpu.make_async_remote_copy(
            tsend, trecv.at[me], ss.at[0], rs.at[0], device_id={"slide": dest}, device_id_type=MESH
        ).start()
        return carry

    def spread(k, buf, source, send_sem, recv_sem, local_sem):
        slot = buf.at[pl.ds(me * 4, 4)]

        def one(r, carry):
            dest = far_first(r)
            pltpu.make_async_remote_copy(
                source(dest), slot, send_sem.at[k], recv_sem.at[k],
                device_id={"slide": dest}, device_id_type=MESH,
            ).start()
            return carry

        pltpu.make_async_copy(source(me), slot, local_sem.at[k]).start()
        lax.fori_loop(0, N - 1, one, 0)

    def deliver(k, buf, target, send_sem, recv_sem, local_sem):
        landing = target.at[:, my_z, :, columns(my_c, k)]

        def one(r, carry):
            dest = far_first(r)
            pltpu.make_async_remote_copy(
                buf.at[k, pl.ds(dest * 4, 4)], landing, send_sem.at[k], recv_sem.at[k],
                device_id={"slide": dest}, device_id_type=MESH,
            ).start()
            return carry

        pltpu.make_async_copy(buf.at[k, pl.ds(me * 4, 4)], landing, local_sem.at[k]).start()
        lax.fori_loop(0, N - 1, one, 0)

    def arrived(k, recv_sem, local_sem):
        await_bytes(s2.at[0, pl.ds(0, 60)], recv_sem.at[k])
        await_bytes(s2.at[0, pl.ds(0, 4)], local_sem.at[k])

    def choose(k, row, source, target):
        def one(i, carry):
            target[k, i] = source[tabs[row, i]]
            return carry

        lax.fori_loop(0, 4 * N, one, 0, unroll=8)

    lax.fori_loop(1, N, send_table, 0)
    def spread_in(k):
        spread(k, r1[k], lambda dest: og_hbm.at[:, dest // 2, :, columns(dest % 2, k)], p1s, p1r, p1l)

    spread_in(0)

    first = lax.broadcasted_iota(jnp.int32, (32, LANES), 1) < HS

    def dilate(ref, pair):
        return jnp.where(
            first,
            ref[pl.ds(2 * pair, 32, stride=R), :],
            ref[pl.ds(2 * pair + 1, 32, stride=R), :],
        )

    loads[0].wait()
    for pair in AHEAD:
        tmp[pair % 4] = ogv[:, :, :, pair * LANES : (pair + 1) * LANES].reshape(ROWS, LANES).astype(F32)
        picked = dilate(tmp.at[pair % 4], pair)
        up, cols = 8 * (pair // 3), slice((pair % 3 - 1) * LANES, (pair % 3) * LANES)
        for t in range(4):
            ogf[t, up : up + 8, cols] = picked[8 * t : 8 * t + 8]
    ogd[...] = ogf[...].astype(BF)

    def pick_slot(dest, carry):
        slot = jnp.int32(0)
        for t in range(4):
            slot = jnp.where((moves_ref[0, t] == dest) & (moves_ref[1, t] < 4), t, slot)
        sd[dest] = ogd[slot]
        return carry

    lax.fori_loop(0, N, pick_slot, 0)

    def send_dilated(r, carry):
        dest = far_first(r)
        pltpu.make_async_remote_copy(
            sd.at[dest], gdr.at[me], ss.at[5], rs.at[5], device_id={"slide": dest}, device_id_type=MESH
        ).start()
        return carry

    lax.fori_loop(0, N - 1, send_dilated, 0)
    pltpu.make_async_copy(sd.at[me], gdr.at[me], ls.at[5]).start()
    for k in range(1, CHUNKS):
        spread_in(k)
    for load in loads[6:]:
        load.start()

    for load in loads[1:6]:
        load.wait()
    alive = (lax.broadcasted_iota(jnp.int32, (ROWS, LANES), 0) + seg * ROWS) < count_ref[0]
    def prepare(pair, carry):
        cols = pl.ds(pl.multiple_of(pair * LANES, LANES), LANES)
        query = qv[:, cols].astype(F32) * (HS ** -0.5)
        keys = jnp.where(alive, kv[:, cols].astype(F32), 0.0)
        qv[:, cols] = query.astype(BF)
        kv[:, cols] = keys.astype(BF)
        k_t[pair] = jnp.transpose(keys).astype(BF)
        tmp[0] = query
        tmp[1] = keys
        tmp[2] = vv[:, cols].astype(F32)
        tmp[3] = ov[:, cols].astype(F32)
        for n in range(4):
            em[pair, n] = dilate(tmp.at[n], pair).astype(BF)
        return carry

    lax.fori_loop(0, PAIRS, prepare, 0)

    norms = nv[...].reshape(H, ROWS)
    head_row = lax.broadcasted_iota(jnp.int32, (H, ROWS), 0)
    head_lane = lax.broadcasted_iota(jnp.int32, (H, ROWS), 1)
    rest = jnp.where(head_lane % R == head_row, norms, 0.0)
    fold_row = lax.broadcasted_iota(jnp.int32, (ROWS, LANES), 0)
    fold_lane = lax.broadcasted_iota(jnp.int32, (ROWS, LANES), 1)
    fold = jnp.where(fold_row // R + 32 * (seg % 4) == fold_lane, 1.0, 0.0).astype(BF)
    folded = jnp.zeros((H, LANES), F32)
    for _ in range(3):
        piece = rest.astype(BF)
        folded = folded + dot(piece, fold)
        rest = rest - piece.astype(F32)
    for h in range(H):
        nmsg[h] = jnp.broadcast_to(folded[h : h + 1], (8, LANES))

    def send_head(src, dst, index, head):
        @pl.when(head != seg)
        def _():
            pltpu.make_async_remote_copy(
                src, dst, ss.at[index], rs.at[index], device_id={"seg": head}, device_id_type=MESH
            ).start()

        @pl.when(head == seg)
        def _():
            pltpu.make_async_copy(src, dst, ls.at[index]).start()

    def send_early(r, carry):
        head = lax.rem(seg + r, N)

        @pl.when(head < H)
        def _():
            send_head(em.at[head // 2], ebuf.at[seg], 1, head)
            send_head(nmsg.at[head], nbuf.at[seg], 2, head)

        return carry

    lax.fori_loop(0, N, send_early, 0)

    await_bytes(trecv.at[pl.ds(0, N - 1)], rs.at[0])
    codes = jnp.zeros((1, LANES), jnp.int32)
    for d in range(N):
        codes = codes + trecv[d]
    down = jnp.transpose(jnp.broadcast_to(codes.astype(F32), (LANES, LANES)))
    spot = lax.broadcasted_iota(jnp.int32, (LANES, LANES), 0)
    match = (down.astype(jnp.int32) == lax.broadcasted_iota(jnp.int32, (LANES, LANES), 1)) & (spot < 4 * N)
    inverse = jnp.sum(jnp.where(match, spot - 4 * N, 0), axis=0, keepdims=True) + 4 * N
    sub = lax.broadcasted_iota(jnp.int32, (8, LANES), 0)
    tabv[...] = jnp.clip(
        jnp.where(
            sub == 0, jnp.broadcast_to(inverse, (8, LANES)), jnp.broadcast_to(codes, (8, LANES))
        ),
        0,
        4 * N,
    )
    table_copy = pltpu.make_async_copy(tabv, tabs, ls.at[0])
    table_copy.start()
    table_copy.wait()

    def relay(k):
        arrived(k, p1r, p1l)
        choose(k, 0, r1[k], s2)
        deliver(k, s2, gbuf, p2s, p2r, p2l)

    wide_half = lax.broadcasted_iota(jnp.int32, (ROWS, LANES), 1) // HS

    def local_weights(k):
        def one(u, carry):
            pair = u * CHUNKS + k
            cols = pl.ds(pl.multiple_of(pair * LANES, LANES), LANES)
            query = qv[:, cols]
            for x in range(2):
                masked = jnp.where(wide_half == x, query, jnp.zeros((ROWS, LANES), BF))
                for i in range(2):
                    rows = slice(256 * i, 256 * i + 256)
                    held[2 * pair + x, rows, :] = weigh(kv[rows, cols], masked, nv[2 * pair + x])
            return carry

        lax.fori_loop(0, 2, one, 0)

    local_weights(0)
    local_weights(1)
    relay(0)

    await_bytes(gdr.at[pl.ds(0, N - 1)], rs.at[5])
    await_bytes(gdr.at[0], ls.at[5])
    for b in range(4):
        got = gdr[tabs[0, me * 4 + b] // 4].astype(F32)
        for pair in AHEAD:
            up, cols = 8 * (pair // 3), slice((pair % 3 - 1) * LANES, (pair % 3) * LANES)
            gmf[pair, 8 * b : 8 * b + 8, :] = got[up : up + 8, cols]
    sparse_row = lax.broadcasted_iota(jnp.int32, (32, LANES), 0) * R + seg * ROWS
    for pair in AHEAD:
        position = sparse_row + jnp.where(first, 2 * pair, 2 * pair + 1)
        gm[pair] = jnp.where(position < count_ref[0], gmf[pair], 0.0).astype(BF)

    def send_grads(r, carry):
        head = lax.rem(seg + r, N)

        @pl.when((head < H) & ((head // 2) % CHUNKS != 0))
        def _():
            send_head(gm.at[head // 2], gdbuf.at[seg], 3, head)

        return carry

    lax.fori_loop(0, N, send_grads, 0)

    for k in range(1, CHUNKS):
        relay(k)

    ones_row = lax.broadcasted_iota(jnp.int32, (8, LANES), 0)
    ones_half = lax.broadcasted_iota(jnp.int32, (8, LANES), 1) // HS
    pair_ones = jnp.where(ones_row == ones_half, 1.0, 0.0).astype(BF)

    def sparse_head(index):
        await_bytes(ebuf.at[pl.ds(0, N - 1)], rs.at[1])
        await_bytes(ebuf.at[0], ls.at[1])
        await_bytes(nbuf.at[pl.ds(0, N - 1)], rs.at[2])
        await_bytes(nbuf.at[0], ls.at[2])
        await_bytes(gdbuf.at[pl.ds(0, N - 1)], rs.at[3])
        await_bytes(gdbuf.at[0], ls.at[3])
        mine = wide_half == seg % 2
        zero = jnp.zeros((ROWS, LANES), BF)
        query = jnp.where(mine, ebuf[:, 0].reshape(ROWS, LANES), zero)
        keys = jnp.where(mine, ebuf[:, 1].reshape(ROWS, LANES), zero)
        vals = ebuf[:, 2].reshape(ROWS, LANES)
        outs = ebuf[:, 3].reshape(ROWS, LANES)
        grad = jnp.where(mine, gdbuf[...].reshape(ROWS, LANES), zero)
        norm = jnp.concatenate(
            [
                sum(nbuf[4 * part + i, 0:1, :] for i in range(4))
                for part in range(4)
            ],
            axis=1,
        )
        dots = row_dots(jnp.ones((8, LANES), BF), grad, outs)[0:1]
        query_t, key_sum, value_sum = attend(
            lambda rows: weigh(keys[rows], query, norm), transposed(keys), vals, query, grad, dots
        )
        rsend[:, 0] = (jnp.transpose(query_t) * (HS ** -0.5)).astype(BF).reshape(N, 32, LANES)
        rsend[:, 1] = key_sum.astype(BF).reshape(N, 32, LANES)
        rsend[:, 2] = value_sum.astype(BF).reshape(N, 32, LANES)

        def back(r, carry):
            dest = lax.rem(seg + r, N)
            pltpu.make_async_remote_copy(
                rsend.at[dest], rbuf.at[seg], ss.at[index], rs.at[index],
                device_id={"seg": dest}, device_id_type=MESH,
            ).start()
            return carry

        lax.fori_loop(1, N, back, 0)
        pltpu.make_async_copy(rsend.at[seg], rbuf.at[seg], ls.at[index]).start()

    owner_late = (seg < H) & ((seg // 2) % CHUNKS == 0)
    owner_ahead = (seg < H) & ((seg // 2) % CHUNKS != 0)

    @pl.when(owner_ahead)
    def _():
        sparse_head(4)

    local_weights(CHUNKS - 1)

    def returned(index, count, mine):
        @pl.when(mine)
        def _():
            await_bytes(rbuf.at[pl.ds(0, count - 1)], rs.at[index])
            await_bytes(rbuf.at[0], ls.at[index])

        @pl.when(jnp.logical_not(mine))
        def _():
            await_bytes(rbuf.at[pl.ds(0, count)], rs.at[index])

    def merge(k, slot):
        for u in range(2):
            pair = u * CHUNKS + k
            for n in range(3):
                place = acc.at[k, u, n]
                for x in range(2):
                    rows = pl.ds(2 * pair + x, 32, stride=R)
                    place[rows, :] = place[rows, :] + rbuf[2 * pair + x, n].astype(F32)
                xs[slot, :, (n * 2 + u) * LANES : (n * 2 + u + 1) * LANES] = place[...].astype(BF)

    def chunk(k, carry):
        arrived(k, p2r, p2l)

        @pl.when(k == 0)
        def _():
            for u in range(2):
                pair = u * CHUNKS
                cols = slice(pair * LANES, (pair + 1) * LANES)
                tmp[u] = jnp.where(alive, gbuf[:, :, :, cols].reshape(ROWS, LANES).astype(F32), 0.0)
                gm[pair] = dilate(tmp.at[u], pair).astype(BF)
                send_head(gm.at[pair], gdbuf.at[seg], 3, 2 * pair)
                send_head(gm.at[pair], gdbuf.at[seg], 3, 2 * pair + 1)

        def local_pair(u, inner):
            pair = u * CHUNKS + k
            cols = pl.ds(pl.multiple_of(pair * LANES, LANES), LANES)
            query, vals = qv[:, cols], vv[:, cols]
            grad = jnp.where(
                alive, gbuf[:, :, :, cols].reshape(ROWS, LANES).astype(F32), 0.0
            ).astype(BF)
            zero = jnp.zeros((ROWS, LANES), BF)
            dots = row_dots(pair_ones, grad, ov[:, cols])
            query_parts, key_sum, value_sum = [], None, None
            for x in range(2):
                mine = wide_half == x
                query_t, key_part, value_part = attend(
                    lambda rows, x=x: held[2 * pair + x, rows, :], k_t[pair, x * HS : (x + 1) * HS, :],
                    vals, jnp.where(mine, query, zero), jnp.where(mine, grad, zero), dots[x : x + 1],
                )
                query_parts.append(query_t)
                key_sum = key_part if key_sum is None else key_sum + key_part
                value_sum = value_part if value_sum is None else value_sum + value_part
            acc[k, u, 0] = jnp.transpose(jnp.concatenate(query_parts, axis=0)) * (HS ** -0.5)
            acc[k, u, 1] = key_sum
            acc[k, u, 2] = value_sum
            return inner

        lax.fori_loop(0, 2, local_pair, 0, unroll=True)

        @pl.when((k == 0) & owner_late)
        def _():
            sparse_head(6)

        @pl.when(k == 1)
        def _():
            for load in loads[6:]:
                load.wait()
            returned(4, 8, owner_ahead)
            merge(1, 0)
            total[...] = dot_nt(xs[0], wv[1])

        return carry

    lax.fori_loop(0, CHUNKS, chunk, 0)
    returned(6, 4, owner_late)
    merge(0, 0)
    merge(CHUNKS - 1, 1)

    for k in range(CHUNKS):
        for core in range(2):
            cols = slice(core * HALF + k * LANES, core * HALF + (k + 1) * LANES)
            mixed = total[:, cols] + dot_nt(xs[0], wv[0, cols, :]) + dot_nt(xs[1], wv[CHUNKS - 1, cols, :])
            mix[k, core] = jnp.where(alive, mixed, 0.0).astype(BF).reshape(4, 8, 16, LANES)
        spread(
            k, q1[k], lambda dest, k=k: mix.at[k, dest % 2, :, dest // 2], o1s, o1r, o1l
        )

    for k in range(CHUNKS):
        arrived(k, o1r, o1l)
        choose(k, 4, q1[k], t2)
        deliver(k, t2, out_ref, o2s, o2r, o2l)
    for k in range(CHUNKS):
        arrived(k, o2r, o2l)

    for sems in (p1s, p2s, o1s, o2s):
        for k in range(CHUNKS):
            await_bytes(s2.at[0, pl.ds(0, 60)], sems.at[k])
    await_bytes(trecv.at[pl.ds(0, N - 1)], ss.at[0])
    await_bytes(gdr.at[pl.ds(0, N - 1)], ss.at[5])

    @pl.when(owner_ahead)
    def _():
        await_bytes(rsend.at[pl.ds(0, N - 1)], ss.at[4])

    @pl.when(owner_late)
    def _():
        await_bytes(rsend.at[pl.ds(0, N - 1)], ss.at[6])

    @pl.when(seg < H)
    def _():
        await_bytes(ebuf.at[pl.ds(0, H - 1)], ss.at[1])
        await_bytes(nbuf.at[pl.ds(0, H - 1)], ss.at[2])
        await_bytes(gdbuf.at[pl.ds(0, H - 1)], ss.at[3])

    @pl.when(seg >= H)
    def _():
        await_bytes(ebuf.at[pl.ds(0, H)], ss.at[1])
        await_bytes(nbuf.at[pl.ds(0, H)], ss.at[2])
        await_bytes(gdbuf.at[pl.ds(0, H)], ss.at[3])


def shards(counts, moves, queries, key_rows, values, forward_out, log_norms, out_grads, weights):
    dma = pltpu.SemaphoreType.DMA
    vmem = pltpu.VMEM
    hbm_spec = pl.BlockSpec(memory_space=pltpu.HBM)
    smem_spec = pl.BlockSpec(memory_space=pltpu.SMEM)
    scratch = [
        *[vmem((ROWS, D), BF)] * 4,
        vmem((H, 1, ROWS), F32),
        vmem((CHUNKS, D, D), BF),
        vmem((PAIRS, LANES, ROWS), BF),
        vmem((1, LANES), jnp.int32),
        vmem((N, 1, LANES), jnp.int32),
        vmem((8, LANES), jnp.int32),
        pltpu.SMEM((8, LANES), jnp.int32),
        vmem((4, 8, 16, D), BF),
        vmem((4, 16, AHEAD_COLS), F32),
        vmem((4, 16, AHEAD_COLS), BF),
        vmem((N, 16, AHEAD_COLS), BF),
        vmem((N + 1, 16, AHEAD_COLS), BF),
        vmem((PAIRS, 32, LANES), F32),
        *[vmem((68, 16, LANES), BF)] * 3,
        vmem((CHUNKS, 64, 16, LANES), BF),
        vmem((4, 8, 16, D), BF),
        vmem((PAIRS, 4, 32, LANES), BF),
        vmem((N, 4, 32, LANES), BF),
        vmem((H, 8, LANES), F32),
        vmem((N, 8, LANES), F32),
        vmem((PAIRS, 32, LANES), BF),
        vmem((N, 32, LANES), BF),
        vmem((N, 3, 32, LANES), BF),
        vmem((H, 3, 32, LANES), BF),
        vmem((H, ROWS, ROWS), F32),
        vmem((4, ROWS, LANES), F32),
        vmem((CHUNKS, 2, 3, ROWS, LANES), F32),
        vmem((2, ROWS, D), BF),
        vmem((ROWS, D), F32),
        vmem((CHUNKS, 2, 4, 8, 16, LANES), BF),
        *[vmem((68, 16, LANES), BF)] * 3,
        vmem((CHUNKS, 64, 16, LANES), BF),
        dma((7,)),
        *[dma((CHUNKS,))] * 12,
        *[dma((7,))] * 3,
    ]
    result = pl.pallas_call(
        kernel,
        out_shape=jax.ShapeDtypeStruct((4, 8, 16, D), BF),
        in_specs=[smem_spec, smem_spec] + [hbm_spec] * 7,
        out_specs=hbm_spec,
        scratch_shapes=scratch,
        compiler_params=pltpu.CompilerParams(
            collective_id=0, has_side_effects=True, vmem_limit_bytes=56 * 1024 * 1024
        ),
        name="dilated_backward",
    )(
        counts,
        moves[0, 0],
        queries[0],
        key_rows[0],
        values[0],
        forward_out[0],
        jnp.transpose(log_norms, (1, 0, 2)),
        out_grads[0].reshape(4, 8, 16, D),
        weights,
    )
    return result.reshape(1, ROWS, D)


def solution(mesh):
    return jax.shard_map(
        shards,
        mesh=mesh,
        in_specs=(
            P("slide"),
            P("slide", "seg", None, None),
            P("slide", "seg", None),
            P("slide", "seg", None),
            P("slide", "seg", None),
            P("slide", "seg", None),
            P("slide", None, "seg"),
            P("slide", "seg", None),
            P(),
        ),
        out_specs=P("slide", "seg", None),
        check_vma=False,
    )
```

```python
import jax
import jax.numpy as jnp
from jax import lax
from jax.experimental import pallas as pl
from jax.experimental.pallas import tpu as pltpu
from jax.sharding import PartitionSpec as P

D = 768
H = 12
R = 16
BLK = 128
ROWS = 512
HS = D // H
LANES = 128
PAIRS = D // LANES
N = 16
CHUNKS = 3
HALF = D // 2
AHEAD = (1, 2, 4, 5)
AHEAD_COLS = 2 * LANES
BF = jnp.bfloat16
F32 = jnp.float32
MESH = pl.DeviceIdType.MESH


def dot(a, b):
    return jnp.dot(a, b, preferred_element_type=F32)


def dot_nt(a, b):
    return lax.dot_general(a, b, (((1,), (1,)), ((), ())), preferred_element_type=F32)


def await_bytes(ref, sem):
    pltpu.make_async_copy(ref, ref, sem).wait()


def transposed(x):
    return jnp.transpose(x.astype(F32)).astype(BF)


def row_dots(ones, grads, outs):
    product = grads.astype(F32) * outs.astype(F32)
    high = product.astype(BF)
    low = (product - high.astype(F32)).astype(BF)
    return dot_nt(ones, high) + dot_nt(ones, low)


def weigh(keys, query, norm):
    return jnp.exp(dot_nt(keys, query) - norm)


def attend(weights_of, keys_t, vals, query, grad, dots):
    value_parts, key_parts, query_t = [], [], None
    for i in range(2):
        rows = slice(256 * i, 256 * i + 256)
        weights = weights_of(rows)
        slopes = dot_nt(vals[rows], grad)
        scores = (weights * (slopes - dots)).astype(BF)
        value_parts.append(dot(weights.astype(BF), grad))
        key_parts.append(dot(scores, query))
        part = dot(keys_t[:, rows], scores)
        query_t = part if query_t is None else query_t + part
    return query_t, jnp.concatenate(key_parts, axis=0), jnp.concatenate(value_parts, axis=0)


def kernel(
    count_ref, moves_ref, q_hbm, k_hbm, v_hbm, o_hbm, norm_hbm, og_hbm, w_hbm, out_ref,
    qv, kv, vv, ov, nv, wv, k_t, tsend, trecv, tabv, tabs,
    ogv, ogf, ogd, sd, gdr, gmf,
    r1a, r1b, r1c, s2, gbuf, em, ebuf, nmsg, nbuf, gm, gdbuf, rsend, rbuf, held, tmp, acc, xs, total, mix,
    q1a, q1b, q1c, t2, in_sem, p1s, p1r, p1l, p2s, p2r, p2l, o1s, o1r, o1l, o2s, o2r, o2l,
    ss, rs, ls,
):
    me = lax.axis_index("slide")
    seg = lax.axis_index("seg")
    my_z, my_c = me // 2, me % 2
    r1, q1 = (r1a, r1b, r1c), (q1a, q1b, q1c)

    barrier = pltpu.get_barrier_semaphore()

    def greet(r, carry):
        pl.semaphore_signal(
            barrier, inc=1, device_id={"slide": lax.rem(me + r, N)}, device_id_type=MESH
        )
        pl.semaphore_signal(
            barrier, inc=1, device_id={"seg": lax.rem(seg + r, N)}, device_id_type=MESH
        )
        return carry

    lax.fori_loop(1, N, greet, 0)

    loads = [
        pltpu.make_async_copy(src, dst, in_sem.at[i])
        for i, (src, dst) in enumerate(
            (
                (og_hbm, ogv), (q_hbm, qv), (k_hbm, kv), (v_hbm, vv), (o_hbm, ov),
                (norm_hbm, nv),
            )
        )
    ]
    for k in range(CHUNKS):
        for n in range(3):
            for u in range(2):
                loads.append(
                    pltpu.make_async_copy(
                        w_hbm.at[:, pl.ds(n * D + u * HALF + k * LANES, LANES)],
                        wv.at[k, :, pl.ds((n * 2 + u) * LANES, LANES)],
                        in_sem.at[6],
                    )
                )
    for load in loads[:6]:
        load.start()

    lane = lax.broadcasted_iota(jnp.int32, (1, LANES), 1)
    table = jnp.zeros((1, LANES), jnp.int32)
    for t in range(4):
        block = moves_ref[1, t]
        code = jnp.where(block < 4, moves_ref[0, t] * 4 + block, 4 * N)
        table = jnp.where(lane == me * 4 + t, code, table)
    tsend[...] = table
    trecv[me] = table
    for buf in r1 + q1:
        buf[64:68] = jnp.zeros((4, 16, LANES), BF)
    gdr[N] = jnp.zeros((16, AHEAD_COLS), BF)

    pl.semaphore_wait(barrier, 2 * (N - 1))

    def far_first(r):
        step = (r // 2 + 1) // 2
        shift = jnp.where((r // 2) % 2 == 1, 4 - step, 4 + step)
        z = jnp.where(r == 14, my_z, lax.rem(my_z + shift, N // 2))
        return z * 2 + jnp.where(r == 14, 1 - my_c, lax.rem(my_c + r, 2))

    def columns(core, k):
        return pl.ds(pl.multiple_of(core * HALF + k * LANES, LANES), LANES)

    def send_table(r, carry):
        dest = lax.rem(me + r, N)
        pltpu.make_async_remote_copy(
            tsend, trecv.at[me], ss.at[0], rs.at[0], device_id={"slide": dest}, device_id_type=MESH
        ).start()
        return carry

    def spread(k, buf, source, send_sem, recv_sem, local_sem):
        slot = buf.at[pl.ds(me * 4, 4)]

        def one(r, carry):
            dest = far_first(r)
            pltpu.make_async_remote_copy(
                source(dest), slot, send_sem.at[k], recv_sem.at[k],
                device_id={"slide": dest}, device_id_type=MESH,
            ).start()
            return carry

        pltpu.make_async_copy(source(me), slot, local_sem.at[k]).start()
        lax.fori_loop(0, N - 1, one, 0)

    def deliver(k, buf, target, send_sem, recv_sem, local_sem):
        landing = target.at[:, my_z, :, columns(my_c, k)]

        def one(r, carry):
            dest = far_first(r)
            pltpu.make_async_remote_copy(
                buf.at[k, pl.ds(dest * 4, 4)], landing, send_sem.at[k], recv_sem.at[k],
                device_id={"slide": dest}, device_id_type=MESH,
            ).start()
            return carry

        pltpu.make_async_copy(buf.at[k, pl.ds(me * 4, 4)], landing, local_sem.at[k]).start()
        lax.fori_loop(0, N - 1, one, 0)

    def arrived(k, recv_sem, local_sem):
        await_bytes(s2.at[0, pl.ds(0, 60)], recv_sem.at[k])
        await_bytes(s2.at[0, pl.ds(0, 4)], local_sem.at[k])

    def choose(k, row, source, target):
        def one(i, carry):
            target[k, i] = source[tabs[row, i]]
            return carry

        lax.fori_loop(0, 4 * N, one, 0, unroll=8)

    lax.fori_loop(1, N, send_table, 0)
    def spread_in(k):
        spread(k, r1[k], lambda dest: og_hbm.at[:, dest // 2, :, columns(dest % 2, k)], p1s, p1r, p1l)

    spread_in(0)

    first = lax.broadcasted_iota(jnp.int32, (32, LANES), 1) < HS

    def dilate(ref, pair):
        return jnp.where(
            first,
            ref[pl.ds(2 * pair, 32, stride=R), :],
            ref[pl.ds(2 * pair + 1, 32, stride=R), :],
        )

    loads[0].wait()
    for pair in AHEAD:
        tmp[pair % 4, :ROWS] = ogv[:, :, :, pair * LANES : (pair + 1) * LANES].reshape(ROWS, LANES).astype(F32)
        picked = dilate(tmp.at[pair % 4], pair)
        up, cols = 8 * (pair // 3), slice((pair % 3 - 1) * LANES, (pair % 3) * LANES)
        for t in range(4):
            ogf[t, up : up + 8, cols] = picked[8 * t : 8 * t + 8]
    ogd[...] = ogf[...].astype(BF)

    def pick_slot(dest, carry):
        slot = jnp.int32(0)
        for t in range(4):
            slot = jnp.where((moves_ref[0, t] == dest) & (moves_ref[1, t] < 4), t, slot)
        sd[dest] = ogd[slot]
        return carry

    lax.fori_loop(0, N, pick_slot, 0)

    def send_dilated(r, carry):
        dest = far_first(r)
        pltpu.make_async_remote_copy(
            sd.at[dest], gdr.at[me], ss.at[5], rs.at[5], device_id={"slide": dest}, device_id_type=MESH
        ).start()
        return carry

    lax.fori_loop(0, N - 1, send_dilated, 0)
    pltpu.make_async_copy(sd.at[me], gdr.at[me], ls.at[5]).start()
    for k in range(1, CHUNKS):
        spread_in(k)
    for load in loads[6:]:
        load.start()

    for load in loads[1:6]:
        load.wait()
    alive = (lax.broadcasted_iota(jnp.int32, (ROWS, LANES), 0) + seg * ROWS) < count_ref[0]
    def prepare(pair, carry):
        cols = pl.ds(pl.multiple_of(pair * LANES, LANES), LANES)
        query = qv[:, cols].astype(F32) * (HS ** -0.5)
        keys = jnp.where(alive, kv[:, cols].astype(F32), 0.0)
        qv[:, cols] = query.astype(BF)
        kv[:, cols] = keys.astype(BF)
        k_t[pair] = jnp.transpose(keys).astype(BF)
        tmp[0, :ROWS] = query
        tmp[1, :ROWS] = keys
        tmp[2, :ROWS] = vv[:, cols].astype(F32)
        tmp[3, :ROWS] = ov[:, cols].astype(F32)
        for n in range(4):
            em[pair, n] = dilate(tmp.at[n], pair).astype(BF)
        return carry

    lax.fori_loop(0, PAIRS, prepare, 0)

    norms = nv[...].reshape(H, ROWS)
    head_row = lax.broadcasted_iota(jnp.int32, (H, ROWS), 0)
    head_lane = lax.broadcasted_iota(jnp.int32, (H, ROWS), 1)
    rest = jnp.where(head_lane % R == head_row, norms, 0.0)
    fold_row = lax.broadcasted_iota(jnp.int32, (ROWS, LANES), 0)
    fold_lane = lax.broadcasted_iota(jnp.int32, (ROWS, LANES), 1)
    fold = jnp.where(fold_row // R + 32 * (seg % 4) == fold_lane, 1.0, 0.0).astype(BF)
    folded = jnp.zeros((H, LANES), F32)
    for _ in range(3):
        piece = rest.astype(BF)
        folded = folded + dot(piece, fold)
        rest = rest - piece.astype(F32)
    for h in range(H):
        nmsg[h] = jnp.broadcast_to(folded[h : h + 1], (8, LANES))

    def send_head(src, dst, index, head):
        @pl.when(head != seg)
        def _():
            pltpu.make_async_remote_copy(
                src, dst, ss.at[index], rs.at[index], device_id={"seg": head}, device_id_type=MESH
            ).start()

        @pl.when(head == seg)
        def _():
            pltpu.make_async_copy(src, dst, ls.at[index]).start()

    def send_early(r, carry):
        head = lax.rem(seg + r, N)

        @pl.when(head < H)
        def _():
            send_head(em.at[head // 2], ebuf.at[seg], 1, head)
            send_head(nmsg.at[head], nbuf.at[seg], 2, head)

        return carry

    lax.fori_loop(0, N, send_early, 0)

    await_bytes(trecv.at[pl.ds(0, N - 1)], rs.at[0])
    codes = jnp.zeros((1, LANES), jnp.int32)
    for d in range(N):
        codes = codes + trecv[d]
    down = jnp.transpose(jnp.broadcast_to(codes.astype(F32), (LANES, LANES)))
    spot = lax.broadcasted_iota(jnp.int32, (LANES, LANES), 0)
    match = (down.astype(jnp.int32) == lax.broadcasted_iota(jnp.int32, (LANES, LANES), 1)) & (spot < 4 * N)
    inverse = jnp.sum(jnp.where(match, spot - 4 * N, 0), axis=0, keepdims=True) + 4 * N
    sub = lax.broadcasted_iota(jnp.int32, (8, LANES), 0)
    tabv[...] = jnp.clip(
        jnp.where(
            sub == 0, jnp.broadcast_to(inverse, (8, LANES)), jnp.broadcast_to(codes, (8, LANES))
        ),
        0,
        4 * N,
    )
    table_copy = pltpu.make_async_copy(tabv, tabs, ls.at[0])
    table_copy.start()
    table_copy.wait()

    def relay(k):
        arrived(k, p1r, p1l)
        choose(k, 0, r1[k], s2)
        deliver(k, s2, gbuf, p2s, p2r, p2l)

    wide_half = lax.broadcasted_iota(jnp.int32, (ROWS, LANES), 1) // HS

    def local_weights(k):
        def one(u, carry):
            pair = u * CHUNKS + k
            cols = pl.ds(pl.multiple_of(pair * LANES, LANES), LANES)
            query = qv[:, cols]
            for x in range(2):
                masked = jnp.where(wide_half == x, query, jnp.zeros((ROWS, LANES), BF))
                for i in range(2):
                    rows = slice(256 * i, 256 * i + 256)
                    held[2 * pair + x, rows, :] = weigh(kv[rows, cols], masked, nv[2 * pair + x])
            return carry

        lax.fori_loop(0, 2, one, 0)

    local_weights(0)
    local_weights(1)
    relay(0)

    await_bytes(gdr.at[pl.ds(0, N - 1)], rs.at[5])
    await_bytes(gdr.at[0], ls.at[5])
    for b in range(4):
        got = gdr[tabs[0, me * 4 + b] // 4].astype(F32)
        for pair in AHEAD:
            up, cols = 8 * (pair // 3), slice((pair % 3 - 1) * LANES, (pair % 3) * LANES)
            gmf[pair, 8 * b : 8 * b + 8, :] = got[up : up + 8, cols]
    sparse_row = lax.broadcasted_iota(jnp.int32, (32, LANES), 0) * R + seg * ROWS
    for pair in AHEAD:
        position = sparse_row + jnp.where(first, 2 * pair, 2 * pair + 1)
        gm[pair] = jnp.where(position < count_ref[0], gmf[pair], 0.0).astype(BF)

    def send_grads(r, carry):
        head = lax.rem(seg + r, N)

        @pl.when((head < H) & ((head // 2) % CHUNKS != 0))
        def _():
            send_head(gm.at[head // 2], gdbuf.at[seg], 3, head)

        return carry

    lax.fori_loop(0, N, send_grads, 0)

    for k in range(1, CHUNKS):
        relay(k)

    ones_row = lax.broadcasted_iota(jnp.int32, (8, LANES), 0)
    ones_half = lax.broadcasted_iota(jnp.int32, (8, LANES), 1) // HS
    pair_ones = jnp.where(ones_row == ones_half, 1.0, 0.0).astype(BF)

    def sparse_head(index):
        await_bytes(ebuf.at[pl.ds(0, N - 1)], rs.at[1])
        await_bytes(ebuf.at[0], ls.at[1])
        await_bytes(nbuf.at[pl.ds(0, N - 1)], rs.at[2])
        await_bytes(nbuf.at[0], ls.at[2])
        await_bytes(gdbuf.at[pl.ds(0, N - 1)], rs.at[3])
        await_bytes(gdbuf.at[0], ls.at[3])
        mine = wide_half == seg % 2
        zero = jnp.zeros((ROWS, LANES), BF)
        query = jnp.where(mine, ebuf[:, 0].reshape(ROWS, LANES), zero)
        keys = jnp.where(mine, ebuf[:, 1].reshape(ROWS, LANES), zero)
        vals = ebuf[:, 2].reshape(ROWS, LANES)
        outs = ebuf[:, 3].reshape(ROWS, LANES)
        grad = jnp.where(mine, gdbuf[...].reshape(ROWS, LANES), zero)
        norm = jnp.concatenate(
            [
                sum(nbuf[4 * part + i, 0:1, :] for i in range(4))
                for part in range(4)
            ],
            axis=1,
        )
        dots = row_dots(jnp.ones((8, LANES), BF), grad, outs)[0:1]
        query_t, key_sum, value_sum = attend(
            lambda rows: weigh(keys[rows], query, norm), transposed(keys), vals, query, grad, dots
        )
        rsend[:, 0] = (jnp.transpose(query_t) * (HS ** -0.5)).astype(BF).reshape(N, 32, LANES)
        rsend[:, 1] = key_sum.astype(BF).reshape(N, 32, LANES)
        rsend[:, 2] = value_sum.astype(BF).reshape(N, 32, LANES)

        def back(r, carry):
            dest = lax.rem(seg + r, N)
            pltpu.make_async_remote_copy(
                rsend.at[dest], rbuf.at[seg], ss.at[index], rs.at[index],
                device_id={"seg": dest}, device_id_type=MESH,
            ).start()
            return carry

        lax.fori_loop(1, N, back, 0)
        pltpu.make_async_copy(rsend.at[seg], rbuf.at[seg], ls.at[index]).start()

    owner_late = (seg < H) & ((seg // 2) % CHUNKS == 0)
    owner_ahead = (seg < H) & ((seg // 2) % CHUNKS != 0)

    @pl.when(owner_ahead)
    def _():
        sparse_head(4)

    local_weights(CHUNKS - 1)

    def returned(index, count, mine):
        @pl.when(mine)
        def _():
            await_bytes(rbuf.at[pl.ds(0, count - 1)], rs.at[index])
            await_bytes(rbuf.at[0], ls.at[index])

        @pl.when(jnp.logical_not(mine))
        def _():
            await_bytes(rbuf.at[pl.ds(0, count)], rs.at[index])

    def merge(k, slot):
        for u in range(2):
            pair = u * CHUNKS + k
            for n in range(3):
                place = acc.at[k, u, n]
                for x in range(2):
                    rows = pl.ds(2 * pair + x, 32, stride=R)
                    place[rows, :] = place[rows, :] + rbuf[2 * pair + x, n].astype(F32)
                xs[slot, :, (n * 2 + u) * LANES : (n * 2 + u + 1) * LANES] = place[:ROWS, :].astype(BF)

    def chunk(k, carry):
        arrived(k, p2r, p2l)

        @pl.when(k == 0)
        def _():
            for u in range(2):
                pair = u * CHUNKS
                cols = slice(pair * LANES, (pair + 1) * LANES)
                tmp[u, :ROWS] = jnp.where(alive, gbuf[:, :, :, cols].reshape(ROWS, LANES).astype(F32), 0.0)
                gm[pair] = dilate(tmp.at[u], pair).astype(BF)
                send_head(gm.at[pair], gdbuf.at[seg], 3, 2 * pair)
                send_head(gm.at[pair], gdbuf.at[seg], 3, 2 * pair + 1)

        def local_pair(u, inner):
            pair = u * CHUNKS + k
            cols = pl.ds(pl.multiple_of(pair * LANES, LANES), LANES)
            query, vals = qv[:, cols], vv[:, cols]
            grad = jnp.where(
                alive, gbuf[:, :, :, cols].reshape(ROWS, LANES).astype(F32), 0.0
            ).astype(BF)
            zero = jnp.zeros((ROWS, LANES), BF)
            dots = row_dots(pair_ones, grad, ov[:, cols])
            query_parts, key_sum, value_sum = [], None, None
            for x in range(2):
                mine = wide_half == x
                query_t, key_part, value_part = attend(
                    lambda rows, x=x: held[2 * pair + x, rows, :], k_t[pair, x * HS : (x + 1) * HS, :],
                    vals, jnp.where(mine, query, zero), jnp.where(mine, grad, zero), dots[x : x + 1],
                )
                query_parts.append(query_t)
                key_sum = key_part if key_sum is None else key_sum + key_part
                value_sum = value_part if value_sum is None else value_sum + value_part
            acc[k, u, 0, :ROWS] = jnp.transpose(jnp.concatenate(query_parts, axis=0)) * (HS ** -0.5)
            acc[k, u, 1, :ROWS] = key_sum
            acc[k, u, 2, :ROWS] = value_sum
            return inner

        lax.fori_loop(0, 2, local_pair, 0, unroll=True)

        @pl.when((k == 0) & owner_late)
        def _():
            sparse_head(6)

        @pl.when(k == 1)
        def _():
            for load in loads[6:]:
                load.wait()
            returned(4, 8, owner_ahead)
            merge(1, 0)
            total[...] = dot_nt(xs[0], wv[1])

        return carry

    lax.fori_loop(0, CHUNKS, chunk, 0)
    returned(6, 4, owner_late)
    merge(0, 0)
    merge(CHUNKS - 1, 1)

    for k in range(CHUNKS):
        for core in range(2):
            cols = slice(core * HALF + k * LANES, core * HALF + (k + 1) * LANES)
            mixed = total[:, cols] + dot_nt(xs[0], wv[0, cols, :]) + dot_nt(xs[1], wv[CHUNKS - 1, cols, :])
            mix[k, core] = jnp.where(alive, mixed, 0.0).astype(BF).reshape(4, 8, 16, LANES)
        spread(
            k, q1[k], lambda dest, k=k: mix.at[k, dest % 2, :, dest // 2], o1s, o1r, o1l
        )

    for k in range(CHUNKS):
        arrived(k, o1r, o1l)
        choose(k, 4, q1[k], t2)
        deliver(k, t2, out_ref, o2s, o2r, o2l)
    for k in range(CHUNKS):
        arrived(k, o2r, o2l)

    for sems in (p1s, p2s, o1s, o2s):
        for k in range(CHUNKS):
            await_bytes(s2.at[0, pl.ds(0, 60)], sems.at[k])
    await_bytes(trecv.at[pl.ds(0, N - 1)], ss.at[0])
    await_bytes(gdr.at[pl.ds(0, N - 1)], ss.at[5])

    @pl.when(owner_ahead)
    def _():
        await_bytes(rsend.at[pl.ds(0, N - 1)], ss.at[4])

    @pl.when(owner_late)
    def _():
        await_bytes(rsend.at[pl.ds(0, N - 1)], ss.at[6])

    @pl.when(seg < H)
    def _():
        await_bytes(ebuf.at[pl.ds(0, H - 1)], ss.at[1])
        await_bytes(nbuf.at[pl.ds(0, H - 1)], ss.at[2])
        await_bytes(gdbuf.at[pl.ds(0, H - 1)], ss.at[3])

    @pl.when(seg >= H)
    def _():
        await_bytes(ebuf.at[pl.ds(0, H)], ss.at[1])
        await_bytes(nbuf.at[pl.ds(0, H)], ss.at[2])
        await_bytes(gdbuf.at[pl.ds(0, H)], ss.at[3])


def shards(counts, moves, queries, key_rows, values, forward_out, log_norms, out_grads, weights):
    dma = pltpu.SemaphoreType.DMA
    vmem = pltpu.VMEM
    hbm_spec = pl.BlockSpec(memory_space=pltpu.HBM)
    smem_spec = pl.BlockSpec(memory_space=pltpu.SMEM)
    scratch = [
        *[vmem((ROWS, D), BF)] * 4,
        vmem((H, 1, ROWS), F32),
        vmem((CHUNKS, D, D), BF),
        vmem((PAIRS, LANES, ROWS), BF),
        vmem((1, LANES), jnp.int32),
        vmem((N, 1, LANES), jnp.int32),
        vmem((8, LANES), jnp.int32),
        pltpu.SMEM((8, LANES), jnp.int32),
        vmem((4, 8, 16, D), BF),
        vmem((4, 16, AHEAD_COLS), F32),
        vmem((4, 16, AHEAD_COLS), BF),
        vmem((N, 16, AHEAD_COLS), BF),
        vmem((N + 1, 16, AHEAD_COLS), BF),
        vmem((PAIRS, 32, LANES), F32),
        *[vmem((68, 16, LANES), BF)] * 3,
        vmem((CHUNKS, 64, 16, LANES), BF),
        vmem((4, 8, 16, D), BF),
        vmem((PAIRS, 4, 32, LANES), BF),
        vmem((N, 4, 32, LANES), BF),
        vmem((H, 8, LANES), F32),
        vmem((N, 8, LANES), F32),
        vmem((PAIRS, 32, LANES), BF),
        vmem((N, 32, LANES), BF),
        vmem((N, 3, 32, LANES), BF),
        vmem((H, 3, 32, LANES), BF),
        vmem((H, ROWS, ROWS), F32),
        vmem((4, ROWS + R, LANES), F32),
        vmem((CHUNKS, 2, 3, ROWS + R, LANES), F32),
        vmem((2, ROWS, D), BF),
        vmem((ROWS, D), F32),
        vmem((CHUNKS, 2, 4, 8, 16, LANES), BF),
        *[vmem((68, 16, LANES), BF)] * 3,
        vmem((CHUNKS, 64, 16, LANES), BF),
        dma((7,)),
        *[dma((CHUNKS,))] * 12,
        *[dma((7,))] * 3,
    ]
    result = pl.pallas_call(
        kernel,
        out_shape=jax.ShapeDtypeStruct((4, 8, 16, D), BF),
        in_specs=[smem_spec, smem_spec] + [hbm_spec] * 7,
        out_specs=hbm_spec,
        scratch_shapes=scratch,
        compiler_params=pltpu.CompilerParams(
            collective_id=0, has_side_effects=True, vmem_limit_bytes=56 * 1024 * 1024
        ),
        name="dilated_backward",
    )(
        counts,
        moves[0, 0],
        queries[0],
        key_rows[0],
        values[0],
        forward_out[0],
        jnp.transpose(log_norms, (1, 0, 2)),
        out_grads[0].reshape(4, 8, 16, D),
        weights,
    )
    return result.reshape(1, ROWS, D)


def solution(mesh):
    return jax.shard_map(
        shards,
        mesh=mesh,
        in_specs=(
            P("slide"),
            P("slide", "seg", None, None),
            P("slide", "seg", None),
            P("slide", "seg", None),
            P("slide", "seg", None),
            P("slide", "seg", None),
            P("slide", None, "seg"),
            P("slide", "seg", None),
            P(),
        ),
        out_specs=P("slide", "seg", None),
        check_vma=False,
    )
```
